32 devices in a mesh: section: 4 (over y, x), rep: 8 (over z, core).
Axes of the slice: x: 2, y: 2, z: 4, core: 2. Of those that a mesh axis runs over, the one named last changes fastest.
Arguments:
- history: bfloat16 [4, 16, 64, 9216], P('section', 'rep'), may hold values from -6 to 6
- codes: int32 [4, 16, 64, 9216], P('section', 'rep'), may hold values from -128 to 127
- scales: float32 [4, 16, 64], P('section', 'rep'), may hold values from 0.003 to 0.03
- sample_ids: int32 [8, 2], P('rep'), may hold values from 0 to 1, each once within a row
- cotangent: bfloat16 [16, 64, 9216], P('rep'), may hold values from -6 to 6
- ln_gain: float32 [4, 9216], P('section'), may hold values from 0.5 to 1.5
- ln_bias: float32 [4, 9216], P('section'), may hold values from -3 to 3
- down_weight: bfloat16 [4, 9216, 256], P('section', 'rep'), may hold values from -0.1875 to 0.1875
- up_weight: bfloat16 [4, 9216, 256], P('section', 'rep'), may hold values from -0.0625 to 0.0625
Outputs:
- input_grads: bfloat16 [4, 16, 64, 9216], P('section', 'rep')
- adapter_grads: float32 [4, 9216, 512], P('section', 'rep')
The draws below stay inside these ranges and needn't reach their ends.
Inputs may be any that keep to these rules, and one draw needn't show every extreme that they name: `sample_ids`: each replica's row names every history entry of that replica once.
All inputs are finite; a program needn't handle non-finite values.
Results may differ from the reference program's by a relative error of at most 0.038.
Values may be sent and summed in bfloat16 or wider, within the bound.
No kernel may reach another device: no remote copies, remote signals or barrier semaphores. Data moves between devices by JAX's collectives and lax.ppermute only.
A program may use at most 128 MiB of HBM per device.

```python
import math
import jax
import jax.numpy as jnp
from jax import lax

D = 9216
R = 256
MB = 2
TOK_MB = 64
N_SECTION = 4
N_REP = 8


def touch_ends(values, rng, smallest, high):
    index_at = [jax.random.randint(jax.random.fold_in(rng, axis), (), 0, length) for axis, length in enumerate(values.shape)]
    widest = values.shape.index(max(values.shape))
    neighbour = index_at[:widest] + [(index_at[widest] + 1) % values.shape[widest]] + index_at[widest + 1:]
    return values.at[tuple(index_at)].set(smallest).at[tuple(neighbour)].set(high)


def spiked(entries, stream_key, source, target, parts, factor):
    def block_of(position):
        return (jnp.arange(entries.shape[position]) // (entries.shape[position] // parts)).reshape((-1,) + (1,) * (entries.ndim - 1 - position))

    near = jax.random.permutation(stream_key, parts)[block_of(target)]
    second = (block_of(target) + parts // 2) % parts
    return jnp.where((block_of(source) == near) | (block_of(source) == second), factor * entries, entries)


def block_levels(stream_key, extent, shards, smallest, largest):
    gain, own = 1.0, jax.random.fold_in(stream_key, 6)
    for position, parts in shards:
        draws = jnp.exp(jax.random.uniform(jax.random.fold_in(own, position), (parts,), jnp.float32, smallest / len(shards), largest / len(shards)))
        gain = gain * jnp.repeat(draws, extent[position] // parts).reshape([-1 if axis == position else 1 for axis in range(len(extent))])
    return gain


def bell_draw(stream_key, extent, width, limit, split=(), kind=jnp.bfloat16):
    drawn = width * jax.random.normal(stream_key, extent, jnp.float32)
    if split:
        drawn = drawn * block_levels(stream_key, extent, split, -0.22, 0.18)
    return jnp.clip(drawn, -limit, limit).astype(kind)


def gaussian_with(own_key, shape, deviation, bound, shards, heavy, kind=jnp.bfloat16):
    array = deviation * jax.random.normal(own_key, shape, jnp.float32)
    if shards:
        array = array * block_levels(own_key, shape, shards, -0.22, 0.18)
    return jnp.clip(spiked(array, jax.random.fold_in(own_key, 3), *heavy), -bound, bound).astype(kind)


def setup_inputs(seed: int = 0) -> dict:
    streams_of = jax.random.split(jax.random.key(seed), 10)
    history = bell_draw(streams_of[0], (N_SECTION, N_REP * MB, TOK_MB, D), 1.0, 6.0, ((0, 4), (1, 8)))
    codes = touch_ends(jax.random.randint(streams_of[1], (N_SECTION, N_REP * MB, TOK_MB, D), -128, 128), jax.random.fold_in(streams_of[1], 1), -128, 127).astype(jnp.int32)
    scales = jnp.clip(jnp.exp(math.log(0.03) - 2.3025851 * jax.random.uniform(streams_of[2], (N_SECTION, N_REP * MB, TOK_MB), jnp.float32) ** block_levels(streams_of[2], (N_SECTION, N_REP * MB, TOK_MB), ((0, 4), (1, 8)), -0.2, 0.2)), 0.003, 0.03)
    sample_ids = jax.vmap(lambda own: jax.random.permutation(own, MB))(jax.random.split(streams_of[3], N_REP)).reshape((N_REP, MB)).astype(jnp.int32)
    cotangent = gaussian_with(streams_of[4], (N_REP * MB, TOK_MB, D), 1.0, 6.0, ((0, 8),), (0, 2, 8, 2.0))
    ln_gain = jnp.clip(1.0 + 0.1 * jax.random.normal(streams_of[5], (N_SECTION, D), jnp.float32), 0.5, 1.5)
    ln_bias = bell_draw(streams_of[6], (N_SECTION, D), 0.5, 3.0, ((0, 4),), jnp.float32)
    down_weight = bell_draw(streams_of[7], (N_SECTION, D, R), (D // 8) ** -0.5, 0.1875, ((0, 4), (1, 8)))
    up_weight = bell_draw(streams_of[8], (N_SECTION, D, R), D ** -0.5, 0.0625, ((0, 4), (1, 8)))
    return dict(history=history, codes=codes, scales=scales, sample_ids=sample_ids, cotangent=cotangent, ln_gain=ln_gain, ln_bias=ln_bias, down_weight=down_weight, up_weight=up_weight)


EPSILON = 1e-05
HALF_ROOT = 0.7071067811865476
DENSITY = 0.3989422804014327

def unpack_codes(levels):
    return levels.astype(jnp.float32)

def gelu_pair(preact):
    normal_cdf = 0.5 * (1.0 + lax.erf(preact * HALF_ROOT))
    bump = DENSITY * jnp.exp(-0.5 * preact * preact)
    return (preact * normal_cdf, normal_cdf + preact * bump)

def section_inputs(stored, packed, scaling, picks):
    chosen = jnp.take(stored, picks, axis=0).astype(jnp.float32)
    rebuilt = chosen + scaling[..., None] * unpack_codes(packed)
    return rebuilt.astype(jnp.bfloat16).reshape(-1, stored.shape[-1])

def normalize(inputs, gain_row, bias_row):
    values = inputs.astype(jnp.float32)
    centred = values - lax.optimization_barrier(jnp.mean(values, axis=-1, keepdims=True))
    inv_std = lax.rsqrt(lax.optimization_barrier(jnp.mean(centred * centred, axis=-1, keepdims=True)) + EPSILON)
    scaled = centred * inv_std
    normed = (scaled * gain_row + bias_row).astype(jnp.bfloat16)
    return (normed, scaled, inv_std)

def input_grad(out_grad, back, gain_row, scaled, inv_std):
    weighted = back * gain_row
    inner = weighted - lax.optimization_barrier(jnp.mean(weighted, axis=-1, keepdims=True)) - scaled * lax.optimization_barrier(jnp.mean(weighted * scaled, axis=-1, keepdims=True))
    return (out_grad.astype(jnp.float32) + inv_std * inner).astype(jnp.bfloat16)

def contract_rows(left, right):
    return lax.dot_general(left, right, (((0,), (0,)), ((), ())), preferred_element_type=jnp.float32)

def contract_cols(left, right):
    return lax.dot_general(left, right, (((1,), (1,)), ((), ())), preferred_element_type=jnp.float32)

def replica_backward(stored, packed, scaling, picks, out_grad, gain_row, bias_row, w_down, w_up):
    inputs = section_inputs(stored, packed, scaling, picks)
    normed, scaled, inv_std = normalize(inputs, gain_row, bias_row)
    activated, slopes = gelu_pair(jnp.dot(normed, w_down, preferred_element_type=jnp.float32))
    hidden = activated.astype(jnp.bfloat16)
    act_grad = (jnp.dot(out_grad, w_up, preferred_element_type=jnp.float32) * slopes).astype(jnp.bfloat16)
    back = contract_cols(act_grad, w_down)
    result = input_grad(out_grad, back, gain_row, scaled, inv_std)
    terms = jnp.concatenate([contract_rows(normed, act_grad), contract_rows(out_grad, hidden)], axis=1) / TOK_MB
    return (result, terms)

def reference(history, codes, scales, sample_ids, cotangent, ln_gain, ln_bias, down_weight, up_weight):
    stored = history.reshape(N_SECTION, N_REP, MB, TOK_MB, D)
    packed = codes.reshape(N_SECTION, N_REP, MB, TOK_MB, D)
    scaling = scales.reshape(N_SECTION, N_REP, MB, TOK_MB)
    start_grad = cotangent.reshape(N_REP, MB * TOK_MB, D)
    batched = jax.vmap(replica_backward, in_axes=(0, 0, 0, 0, 0, None, None, None, None))

    def per_section(out_grad, section_id):
        results, terms = batched(stored[section_id], packed[section_id], scaling[section_id], sample_ids, out_grad, ln_gain[section_id], ln_bias[section_id], down_weight[section_id], up_weight[section_id])
        rounded = lax.optimization_barrier(terms.astype(jnp.bfloat16))
        summed = lax.optimization_barrier(jnp.sum(rounded.astype(jnp.float32), axis=0))
        return (results, (results, summed))
    _, (grads_in, sums) = lax.scan(per_section, start_grad, jnp.arange(N_SECTION, dtype=jnp.int32), reverse=True)
    return (grads_in.reshape(N_SECTION, N_REP * MB, TOK_MB, D), sums)
```

```python
import functools

import jax
import jax.numpy as jnp
from jax import lax
from jax.experimental import pallas as pl
from jax.experimental.pallas import tpu as pltpu
from jax.sharding import PartitionSpec as P

EPSILON = 1e-05
HALF_ROOT = 0.7071067811865476
DENSITY = 0.3989422804014327


def from_behind(value, axis, steps):
    count = lax.axis_size(axis)
    leading, last = (max(0, -steps), min(count, count - steps))
    return lax.ppermute(value, axis, [(source, source + steps) for source in range(leading, last)])


def unpack_codes(levels):
    return levels.astype(jnp.float32)


def gelu_pair(preact):
    normal_cdf = 0.5 * (1.0 + lax.erf(preact * HALF_ROOT))
    bump = DENSITY * jnp.exp(-0.5 * preact * preact)
    return (preact * normal_cdf, normal_cdf + preact * bump)


def section_inputs(stored, packed, scaling, picks):
    chosen = jnp.take(stored, picks, axis=0).astype(jnp.float32)
    rebuilt = chosen + scaling[..., None] * unpack_codes(packed)
    return rebuilt.astype(jnp.bfloat16).reshape(-1, stored.shape[-1])


def normalize(inputs, gain_row, bias_row):
    values = inputs.astype(jnp.float32)
    centred = values - jnp.mean(values, axis=-1, keepdims=True)
    inv_std = lax.rsqrt(jnp.mean(centred * centred, axis=-1, keepdims=True) + EPSILON)
    scaled = centred * inv_std
    normed = (scaled * gain_row + bias_row).astype(jnp.bfloat16)
    return (normed, scaled, inv_std)


def input_grad(out_grad, back, gain_row, scaled, inv_std):
    weighted = back * gain_row
    inner = (
        weighted
        - jnp.mean(weighted, axis=-1, keepdims=True)
        - scaled * jnp.mean(weighted * scaled, axis=-1, keepdims=True)
    )
    return (out_grad.astype(jnp.float32) + inv_std * inner).astype(jnp.bfloat16)


def contract_rows(left, right):
    return lax.dot_general(
        left, right, (((0,), (0,)), ((), ())), preferred_element_type=jnp.float32
    )


def contract_cols(left, right):
    return lax.dot_general(
        left, right, (((1,), (1,)), ((), ())), preferred_element_type=jnp.float32
    )


def take_rows(source, begin, count):
    return lax.dynamic_slice_in_dim(source, begin, count, 0)


def put_rows(target, active, values, begin):
    older = lax.dynamic_slice_in_dim(target, begin, values.shape[0], 0)
    return lax.dynamic_update_slice_in_dim(target, jnp.where(active, values, older), begin, 0)


def plain_device(
    history, codes, scales, sample_ids, cotangent, ln_gain, ln_bias, down_weight, up_weight
):
    sections = lax.axis_size("section")
    position = lax.axis_index("section")
    w_down, w_up = (
        lax.all_gather(down_weight[0], "rep", axis=0, tiled=True),
        lax.all_gather(up_weight[0], "rep", axis=0, tiled=True),
    )
    inputs = section_inputs(history[0], codes[0], scales[0], sample_ids[0])
    gain_row = ln_gain[0]
    bias_row = ln_bias[0]
    normed, scaled, inv_std = normalize(inputs, gain_row, bias_row)
    activated, slopes = gelu_pair(jnp.dot(normed, w_down, preferred_element_type=jnp.float32))
    hidden = activated.astype(jnp.bfloat16)
    tok_count = cotangent.shape[1]
    row_total = inputs.shape[0]
    model_width = inputs.shape[1]
    rank_pair = 2 * w_down.shape[1]
    seeded = cotangent.reshape(row_total, model_width)
    pieces = 1
    block_size = tok_count // pieces
    blocks = row_total // block_size
    tick_count = blocks + sections - 1

    def advance(tick, carry):
        incoming, produced, running, kept_grad, kept_top = carry
        offset = tick - (sections - 1 - position)
        active = jnp.logical_and(offset >= 0, offset < blocks)
        begin = jnp.clip(offset, 0, blocks - 1) * block_size
        top_grad = take_rows(seeded, begin, block_size)
        out_grad = jnp.where(position == sections - 1, top_grad, incoming)
        slope_rows = take_rows(slopes, begin, block_size)
        scaled_rows = take_rows(scaled, begin, block_size)
        inv_rows = take_rows(inv_std, begin, block_size)
        act_grad = (
            jnp.dot(out_grad, w_up, preferred_element_type=jnp.float32) * slope_rows
        ).astype(jnp.bfloat16)
        back = contract_cols(act_grad, w_down)
        result = input_grad(out_grad, back, gain_row, scaled_rows, inv_rows)
        produced = put_rows(produced, active, result, begin)
        normed_rows = take_rows(normed, begin, block_size)
        hidden_rows = take_rows(hidden, begin, block_size)
        terms = jnp.concatenate(
            [contract_rows(normed_rows, act_grad), contract_rows(out_grad, hidden_rows)], axis=1
        )
        running = running + jnp.where(active, terms, 0.0)
        incoming = from_behind(result, "section", -1)
        return (incoming, produced, running, kept_grad, kept_top)

    start_in = jnp.zeros((block_size, model_width), jnp.bfloat16)
    start_out = jnp.zeros((row_total, model_width), jnp.bfloat16)
    start_sum = jnp.zeros((model_width, rank_pair), jnp.float32)
    start_grad = jnp.zeros((1, 1), jnp.bfloat16)
    start_top = jnp.zeros((1, 1), jnp.bfloat16)
    carry = lax.fori_loop(
        0, tick_count, advance, (start_in, start_out, start_sum, start_grad, start_top)
    )
    produced = carry[1]
    summed = lax.psum_scatter(
        (carry[2] / float(tok_count)).astype(jnp.bfloat16), "rep", scatter_dimension=0, tiled=True
    ).astype(jnp.float32)
    return (produced.reshape(1, row_total // tok_count, tok_count, model_width), summed[None])


VMEM_LIMIT = 16 * 1024 * 1024
F32 = jnp.float32
BF16 = jnp.bfloat16


def run_kernel(body, outs, args, grid=(1,), scalars=(), scratch=(), aliases=None, limit=VMEM_LIMIT):
    def whole(shape):
        return pl.BlockSpec(shape, lambda *_: (0,) * len(shape))

    arrays, in_specs, out_specs, out_shapes = [], [], [], []
    for arg in args:
        if isinstance(arg, tuple) and arg[1] is None:
            arrays.append(arg[0])
            in_specs.append(pl.BlockSpec(memory_space=pltpu.HBM))
        elif isinstance(arg, tuple):
            arrays.append(arg[0])
            in_specs.append(pl.BlockSpec(arg[1], arg[2]))
        else:
            arrays.append(arg)
            in_specs.append(whole(arg.shape))
    for out in outs:
        out_shapes.append(jax.ShapeDtypeStruct(out[0], out[1]))
        out_specs.append(pl.BlockSpec(out[2], out[3]) if len(out) > 2 else whole(out[0]))
    return pl.pallas_call(
        body,
        out_shape=out_shapes,
        grid_spec=pltpu.PrefetchScalarGridSpec(
            num_scalar_prefetch=len(scalars),
            grid=grid,
            in_specs=in_specs,
            out_specs=out_specs,
            scratch_shapes=list(scratch),
        ),
        input_output_aliases=aliases or {},
        compiler_params=pltpu.CompilerParams(vmem_limit_bytes=limit),
        cost_estimate=pl.CostEstimate(flops=0, bytes_accessed=0, transcendentals=0),
    )(*scalars, *arrays)


def regroup_body(
    blocks, picks, hist0, hist1, code0, code1, cot0, cot1, step, own, sent, stats, kept, *, micro, tok
):
    place = pl.program_id(0)
    last = pl.num_programs(0) - 1

    @pl.when(place < last)
    def _():
        for which, (hist, code, cot, out) in enumerate(
            ((hist0, code0, cot0, own), (hist1, code1, cot1, sent))
        ):
            for m in range(micro):
                rows = pl.ds(m * tok, tok)
                rebuilt = hist[picks[m]].astype(F32) + step[m] * code[m].astype(F32)
                rebuilt = rebuilt.astype(BF16)
                out[0, rows, :] = rebuilt
                out[1, rows, :] = cot[m]
                kept[2 * place + which, rows, :] = rebuilt

    @pl.when(place == last)
    def _():
        total, rows, lanes = kept.shape
        width = total * lanes

        def add(index, acc):
            return acc + jnp.sum(kept[index].astype(F32), axis=-1, keepdims=True)

        mean = lax.fori_loop(0, total, add, jnp.zeros((rows, 1), F32)) / width

        def add_square(index, acc):
            centred = kept[index].astype(F32) - mean
            return acc + jnp.sum(centred * centred, axis=-1, keepdims=True)

        var = lax.fori_loop(0, total, add_square, jnp.zeros((rows, 1), F32)) / width
        inv_std = lax.rsqrt(var + EPSILON)
        half = stats.shape[1] // 2
        stats[:, :half] = jnp.broadcast_to(mean, (rows, half))
        stats[:, half:] = jnp.broadcast_to(inv_std, (rows, half))
        lane = lax.broadcasted_iota(jnp.int32, (rows, 128), 1)
        packed = jnp.zeros((rows, 128), F32)
        for index, value in enumerate(bf16_parts(mean) + bf16_parts(inv_std)):
            packed = jnp.where(lane == index, value, packed)
        sent[0, :, :128] = packed.astype(BF16)


def bf16_parts(value):
    parts = []
    for _ in range(3):
        parts.append(value.astype(BF16).astype(F32))
        value = value - parts[-1]
    return parts


def split_stats(stats):
    if len(stats.shape) == 3:
        parts = stats[0].astype(F32)
        return [sum(parts[:, i : i + 1] for i in range(k, k + 3)) for k in (0, 3)]
    half = stats.shape[1] // 2
    return stats[:, 0:1], stats[:, half : half + 1]


def norm_body(blocks, own, sib, stats_own, stats_sib, gain, bias, out):
    tokens = own.shape[1]
    for slot, (values, stats) in enumerate(((own, stats_own), (sib, stats_sib))):
        mean, inv_std = split_stats(stats)
        scaled = (values[0].astype(F32) - mean) * inv_std
        out[slot * tokens : (slot + 1) * tokens, :] = (scaled * gain[...] + bias[...]).astype(BF16)


def as_column(row, lanes):
    turned = jnp.transpose(jnp.broadcast_to(row, (128, row.shape[1])))
    return jnp.concatenate([turned] * (lanes // 128), axis=1)


def step_body(*refs, first, sections):
    refs = refs[1:]
    own, sib, stats_own, stats_sib, gain, bias, down, up, near, far, diag_a, diag_b = refs[:12]
    refs = refs[12:]
    if first:
        old = None
        outs = refs
    else:
        old, outs = refs[:3], refs[3:]
    rank = down.shape[1]
    tokens = own.shape[1]
    weights = down[...]
    gain_row, bias_row = gain[...], bias[...]
    others = [near[...], far[...], jnp.concatenate([diag_a[...], diag_b[...]], axis=0)]
    for slot, (values, stats) in enumerate(((own, stats_own), (sib, stats_sib))):
        mean, inv_std = split_stats(stats)
        inputs = values[0]
        scaled = (inputs.astype(F32) - mean) * inv_std
        normed = (scaled * gain_row + bias_row).astype(BF16)
        pieces = [
            jnp.dot(values[1], up[...], preferred_element_type=F32),
            jnp.dot(normed, weights, preferred_element_type=F32),
        ] + [jnp.dot(inputs, other, preferred_element_type=F32) for other in others]
        for index, piece in enumerate(pieces):
            columns = slice(index * rank, (index + 1) * rank)
            if old is not None:
                piece = piece + old[slot][:, columns]
            outs[slot][:, columns] = piece
    wide = weights.astype(F32)
    gained = wide * as_column(gain_row, rank)
    biased = wide * as_column(bias_row, rank)
    gained_low = gained.astype(BF16)
    cross = outs[2]

    def put(rows, columns, value):
        if old is not None:
            value = value + old[2][rows, columns]
        cross[rows, columns] = value

    for index, other in enumerate(others):
        columns = slice(index * rank, (index + 1) * rank)
        put(slice(0, rank), columns, contract_rows(gained_low, other))
        put(
            slice(rank, rank + 1),
            columns,
            jnp.sum(other.astype(F32), axis=0, keepdims=True),
        )
    put(slice(rank + 1, rank + 2), slice(0, rank), jnp.sum(gained, axis=0, keepdims=True))
    put(slice(rank + 1, rank + 2), slice(rank, 2 * rank), jnp.sum(biased, axis=0, keepdims=True))


def chain_values(pre, slopes, centred, spread, cross, kappa, inv_std, width):
    act_grad = (pre * slopes).astype(BF16)
    wide = act_grad.astype(F32)
    second = jnp.sum(wide * centred, axis=-1, keepdims=True) / width
    return inv_std * (jnp.dot(act_grad, cross, preferred_element_type=F32) - second * spread)


def open_body(
    mine, got, cross, cross_got, stats, small, shared, spread_out, cross_out, kappa_out, near, rest, *, width
):
    rank = near.shape[1]
    total = mine[...] + got[...]
    both = cross[...] + cross_got[...]
    mean, inv_std = split_stats(stats)
    base = total[:, :rank]
    preact = total[:, rank : 2 * rank]
    sums = both[rank : rank + 1, :]
    kappa = both[rank + 1 : rank + 2, :rank]
    beta = both[rank + 1 : rank + 2, rank : 2 * rank]
    activated, slopes = gelu_pair(preact)
    centred = preact - beta
    spread = inv_std * (total[:, 2 * rank :] - mean * sums)
    kappa_column = as_column(kappa, rank)[:, 0:1]
    projected = (both[:rank, :] - kappa_column * (sums / width)).astype(BF16)
    small[:, :rank] = base
    small[:, rank:] = slopes
    shared[:, :rank] = activated
    shared[:, rank:] = centred
    spread_out[...] = spread
    cross_out[...] = projected
    kappa_out[...] = jnp.broadcast_to(kappa, kappa_out.shape)
    values = chain_values(base, slopes, centred, spread, projected, kappa, inv_std, width)
    near[...] = values[:, :rank].astype(BF16)
    rest[...] = values[:, rank:].astype(BF16)


def chain_body(*refs, width, turn):
    small, shared, spread, cross, kappa, stats = refs[:6]
    arrivals, out = refs[6:-1], refs[-1]
    rank = cross.shape[0]
    _, inv_std = split_stats(stats)
    pre = small[:, :rank]
    for arrival in arrivals:
        pre = pre + arrival[:, :rank].astype(F32)
    slopes = small[:, rank:]
    if turn == 3:
        out[...] = (pre * slopes).astype(BF16)
        return
    values = chain_values(
        pre, slopes, shared[:, rank:], spread[...], cross[...], kappa[0:1, :], inv_std, width
    )
    if turn == 1:
        out[:, :rank] = values[:, 2 * rank :].astype(BF16)
        out[:, rank:] = values[:, rank : 2 * rank].astype(BF16)
        return
    passed = arrivals[1][:, rank:].astype(F32) + arrivals[2][:, rank:].astype(F32)
    out[...] = (values[:, :rank] + passed).astype(BF16)


def grad_body(*refs, scale, width, index):
    *refs, held, sems = refs
    columns = pl.ds(index * held.shape[2], held.shape[2])
    copies = [
        pltpu.make_async_copy(source.at[0, :, columns], held.at[slot], sems.at[slot])
        for slot, source in enumerate(refs[1:3])
    ]
    for copy in copies:
        copy.start()
    stats_own, stats_sib, act_own, act_sib, shared_own, shared_sib, kappa = refs[3:10]
    gain, bias, down, term, *grads = refs[10:]
    gain_row, bias_row = gain[...], bias[...]
    weights = down[...]
    rank = weights.shape[1]
    total = None
    for slot, (stats, act, shared) in enumerate(
        ((stats_own, act_own, shared_own), (stats_sib, act_sib, shared_sib))
    ):
        mean, inv_std = split_stats(stats)
        act_grad = act[...]
        wide = act_grad.astype(F32)
        first = jnp.sum(wide * kappa[0:1, :], axis=-1, keepdims=True) / width
        second = jnp.sum(wide * shared[:, rank:], axis=-1, keepdims=True) / width
        copies[slot].wait()
        scaled = (held[slot].astype(F32) - mean) * inv_std
        normed = (scaled * gain_row + bias_row).astype(BF16)
        weighted = contract_cols(act_grad, weights) * gain_row
        tokens = act_grad.shape[0]
        term[slot * tokens : (slot + 1) * tokens, :] = (
            inv_std * (weighted - first - scaled * second)
        ).astype(BF16)
        piece = contract_rows(normed, act_grad)
        total = piece if total is None else total + piece
    for grad in grads:
        grad[...] = (total * scale).astype(BF16)


def ahead_body(normed, act, own, out, *, scale):
    out[...] = own[...].astype(F32) + contract_rows(normed[...], act[...]) * scale


def close_body(*refs, scale, count, index):
    *refs, held, sems = refs
    columns = pl.ds(index * held.shape[2], held.shape[2])
    copies = [
        pltpu.make_async_copy(source.at[1, :, columns], held.at[slot], sems.at[slot])
        for slot, source in enumerate(refs[1:3])
    ]
    for copy in copies:
        copy.start()
    level, _, _, shared_own, shared_sib, term = refs[0:6]
    arrivals = refs[6 : 6 + count]
    mine, theirs, grad = refs[6 + count :]
    rank = grad.shape[1]
    total = None
    for slot, (shared, out) in enumerate(((shared_own, mine), (shared_sib, theirs))):
        tokens = shared.shape[0]
        rows = slice(slot * tokens, (slot + 1) * tokens)
        copies[slot].wait()
        arrived = held[slot].astype(F32)
        for place, arrival in enumerate(arrivals):
            values = arrival[rows, :].astype(F32)
            if place == 0:
                values = jnp.where(level[0] % 2 == 0, values, 0.0)
            arrived = arrived + values
        out_grad = arrived.astype(BF16)
        out[...] = (out_grad.astype(F32) + term[rows, :].astype(F32)).astype(BF16)
        piece = contract_rows(out_grad, shared[:, :rank].astype(BF16))
        total = piece if total is None else total + piece
    grad[...] = (total * scale).astype(BF16)


def place_body(blocks, *refs, count):
    mines, arrived, out = refs[:count], refs[count], refs[-1]
    place = pl.program_id(0)
    for index, source in enumerate(mines):

        @pl.when(place == index)
        def _():
            out[...] = source[...]

    @pl.when(place >= count)
    def _():
        out[...] = arrived[...]


def per_device(
    history, codes, scales, sample_ids, cotangent, ln_gain, ln_bias, down_weight, up_weight
):
    sections = lax.axis_size("section")
    reps = lax.axis_size("rep")
    line = reps // 2
    section = lax.axis_index("section")
    rep = lax.axis_index("rep")
    chip, core = rep // 2, rep % 2
    _, micro, tok, width = history.shape
    tokens = micro * tok
    rows, rank = down_weight.shape[1:]

    def sibling(value):
        return lax.ppermute(value, "rep", [(r, r ^ 1) for r in range(reps)])

    def along(value, steps=1):
        return lax.ppermute(value, "rep", [(r, (r + 2 * steps) % reps) for r in range(reps)])

    def flip(value, mask):
        return lax.ppermute(value, "section", [(s, s ^ mask) for s in range(sections)])

    def after(value, *first):
        return lax.optimization_barrier((value, first))[0]

    chips = (chip - jnp.arange(line, dtype=jnp.int32)) % line
    blocks = jnp.concatenate([2 * chips + core, 2 * chips + 1 - core]).astype(jnp.int32)
    gain, bias = ln_gain, ln_bias

    ups, downs = [up_weight[0]], [down_weight[0]]
    cut = rows // 2

    def both(value):
        return flip(value, 1), flip(value, 2)

    def first_half(near, *first):
        return flip(after(near, *first)[:cut], 2)

    def second_half(far, *first):
        return flip(after(far, *first)[cut:], 1)

    nears = [both(ups[0])]
    ups.append(along(ups[0]))

    def columns(kind):
        return lambda i, blk, ids: (0, 0, blk[kind * line + jnp.minimum(i, line - 1)])

    own, sent, stats = run_kernel(
        functools.partial(regroup_body, micro=micro, tok=tok),
        [
            (
                (2, tokens, line * rows),
                BF16,
                (2, tokens, rows),
                lambda i, *_: (0, 0, jnp.minimum(i, line - 1)),
            ),
            ((2, tokens, (line + 1) * rows), BF16, (2, tokens, rows), lambda i, *_: (0, 0, i)),
            ((tokens, 256), F32),
        ],
        [
            (value, (micro, tok, rows), columns(kind))
            for value in (history[0], codes[0], cotangent)
            for kind in (0, 1)
        ]
        + [scales[0][..., None]],
        grid=(line + 1,),
        scalars=(blocks, sample_ids[0]),
        scratch=[pltpu.VMEM((2 * line, tokens, rows), BF16)],
    )
    sib = sibling(after(sent, *nears[0], ups[1]))
    stats_sib = (sib, (1, tokens, 128), lambda i, *_: (0, 0, line * rows // 128))

    ups.append(along(ups[1]))
    downs.append(along(after(downs[0], ups[1])))
    nears.append(both(ups[1]))
    def part(value, index):
        return (value, (2, tokens, rows), lambda i, *_: (0, 0, index))

    def one(value, kind, index):
        return (value, (1, tokens, rows), lambda i, *_: (kind, 0, index))

    def feature(value, index):
        return (value, (1, rows), lambda i, blk: (0, blk[index]))

    def add_step(sums, index, gathered):
        first = index == 0
        args = [
            part(own, index),
            part(sib, index),
            stats,
            stats_sib,
            feature(gain, index),
            feature(bias, index),
            downs[index],
            ups[index],
            *gathered,
        ]
        shapes = [
            ((tokens, (1 + sections) * rank), F32),
            ((tokens, (1 + sections) * rank), F32),
            ((rank + 8, (sections - 1) * rank), F32),
        ]
        return run_kernel(
            functools.partial(step_body, first=first, sections=sections),
            shapes,
            args + list(sums),
            scalars=(blocks,),
            aliases=None if first else {13 + i: i for i in range(3)},
            limit=28 * 1024 * 1024,
        )

    firsts = [first_half(nears[0][0], *nears[1])]
    ups.append(along(ups[2]))
    downs.append(along(downs[1]))
    nears.append(both(after(ups[2], *nears[1], sib)))
    seconds = [second_half(nears[0][1], *nears[2])]
    firsts.append(first_half(nears[1][0], *nears[2]))
    seconds.append(second_half(nears[1][1], *nears[2]))
    sums = add_step((), 0, nears[0] + (firsts[0], seconds[0]))
    nears.append(both(after(ups[3], *nears[2], *firsts, *seconds, *sums)))
    for index in range(2, line):
        firsts.append(first_half(nears[index][0]))
        seconds.append(second_half(nears[index][1]))
    downs.append(along(downs[2]))
    for index in range(1, line):
        sums = add_step(sums, index, nears[index] + (firsts[index], seconds[index]))
    mine, other, cross = sums
    (normed,) = run_kernel(
        norm_body,
        [((2 * tokens, rows), BF16)],
        [
            one(own, 0, 1),
            one(sib, 0, 1),
            stats,
            stats_sib,
            feature(gain, 1),
            feature(bias, 1),
        ],
        scalars=(blocks,),
    )
    normed_ahead = along(after(normed, mine), -1)

    got, cross_got = sibling(other), sibling(cross)

    apart = sections - 1
    small, shared, spread, projected, kappa, to_next, to_rest = run_kernel(
        functools.partial(open_body, width=width),
        [
            ((tokens, 2 * rank), F32),
            ((tokens, 2 * rank), F32),
            ((tokens, apart * rank), F32),
            ((rank, apart * rank), BF16),
            ((8, rank), F32),
            ((tokens, rank), BF16),
            ((tokens, 2 * rank), BF16),
        ],
        [mine, got, cross, cross_got, stats],
    )
    arrivals = [lax.ppermute(to_next, "section", [(3, 2)])]
    late = lax.ppermute(to_rest, "section", [(3, 1)])
    state = [small, shared, spread, projected, kappa, stats]
    for turn in (1, 2, 3):
        (passed,) = run_kernel(
            functools.partial(chain_body, width=width, turn=turn),
            [((tokens, 2 * rank if turn == 1 else rank), BF16)],
            state + (after(arrivals, normed_ahead) if turn == 3 else arrivals),
        )
        if turn == 1:
            arrivals += [late, lax.ppermute(passed, "section", [(2, 1)])]
        elif turn == 2:
            arrivals += [lax.ppermute(passed, "section", [(1, 0)])]
    act = passed
    act_sib, shared_sib = sibling(act), sibling(shared)

    scale = 1.0 / tok
    level = section.astype(jnp.int32).reshape(1)

    def grad_block(index, act):
        outs = [((2 * tokens, rows), BF16)]
        if index != 1:
            outs.append(((rows, rank), BF16))
        return run_kernel(
            functools.partial(grad_body, scale=scale, width=width, index=index),
            outs,
            [
                (own, None),
                (sib, None),
                stats,
                stats_sib,
                act,
                act_sib,
                shared,
                shared_sib,
                kappa,
                feature(gain, index),
                feature(bias, index),
                downs[index],
            ],
            scalars=(blocks,),
            scratch=[pltpu.VMEM((2, tokens, rows), BF16), pltpu.SemaphoreType.DMA((2,))],
        )

    def close_block(index, arrived):
        return run_kernel(
            functools.partial(close_body, scale=scale, count=len(arrived), index=index),
            [((tokens, rows), BF16), ((tokens, rows), BF16), ((rows, rank), BF16)],
            [(own, None), (sib, None), shared, shared_sib, terms[index], *arrived],
            scalars=(level,),
            scratch=[pltpu.VMEM((2, tokens, rows), BF16), pltpu.SemaphoreType.DMA((2,))],
        )

    terms, down_grads, up_grads, mines, theirs = {}, {}, {}, {}, {}
    (terms[1],) = grad_block(1, act)
    act = after(act, terms[1])
    for index in (2, 3):
        terms[index], *down_grads[index] = grad_block(index, act)

    def add(*values):
        return sum(value.astype(F32) for value in values)

    def pass_on(running, part):
        return along(add(running, part).astype(BF16))

    def scan_open(index):
        return lax.ppermute(terms[index], "section", [(3, 2), (1, 0), (2, 3)])

    def scan_pairs(*pairs):
        return lax.ppermute(terms[1], "section", pairs)

    def scan_sum(index, arrived):
        return add(terms[index], arrived).astype(BF16)

    def scan_more(value):
        return lax.ppermute(value, "section", [(3, 1), (2, 0)])

    opened = {1: scan_pairs((3, 2), (2, 3))}
    beside = scan_pairs((1, 0))
    opened.update({index: scan_open(index) for index in (2, 3)})
    down_ring = along(down_grads[2][0])
    sums = {1: scan_sum(1, after(opened[1], terms[2], terms[3]))}
    more = {1: scan_more(sums[1])}
    down_sum = add(after(down_ring, beside), down_grads[3][0]).astype(BF16)
    down_ring = along(down_sum)
    mines[1], theirs[1], up_grads[1] = close_block(
        1, (opened[1], after(more[1], down_sum), beside)
    )
    up_ring = along(up_grads[1])
    sums[2] = scan_sum(2, after(opened[2], up_grads[1]))
    more[2] = scan_more(sums[2])
    terms[0], *down_grads[0] = grad_block(0, after(act, up_grads[1]))
    opened[0] = scan_open(0)
    sums[3] = scan_sum(3, after(opened[3], sums[2]))
    more[3] = scan_more(sums[3])
    mines[2], theirs[2], up_grads[2] = close_block(
        2, (opened[2], after(more[2], sums[3], down_ring))
    )
    more[0] = scan_more(scan_sum(0, after(opened[0], sums[3], up_grads[2])))
    act_ahead = along(jnp.concatenate(after([act, act_sib], up_grads[2]), axis=0), -1)
    mines[3], theirs[3], up_grads[3] = close_block(3, (opened[3], after(more[3], act_ahead)))
    up_ring = pass_on(up_ring, up_grads[2])
    up_sum = add(up_ring, up_grads[3]).astype(BF16)
    up_ring = along(up_sum)
    def place(first, count, produced):
        sent = [theirs[index] for index in range(first, first + count)]
        arrived = sibling(jnp.concatenate(sent, axis=1) if count > 1 else sent[0])
        args = [mines[index] for index in range(first, first + count)]
        args.append((arrived, (tokens, rows), lambda i, blk: (0, jnp.maximum(i - count, 0))))
        if produced is not None:
            args.append((produced, None))

        def target(i, blk):
            return (0, blk[first + jnp.where(i < count, i, line + i - count)])

        return run_kernel(
            functools.partial(place_body, count=count),
            [((tokens, width), BF16, (tokens, rows), target)],
            args,
            grid=(2 * count,),
            scalars=(blocks,),
            aliases=None if produced is None else {len(args): 0},
        )[0]

    produced = place(1, line - 1, None)
    mines[0], theirs[0], up_grads[0] = close_block(
        0, (opened[0], after(more[0], up_ring, produced))
    )
    produced = place(0, 1, produced)
    (down_own,) = run_kernel(
        functools.partial(ahead_body, scale=scale),
        [((rows, rank), F32)],
        [normed_ahead, act_ahead, after(down_grads[0][0], mines[3])],
    )
    up_sum = add(up_ring, up_grads[0])
    grads = jnp.concatenate([add(down_ring, down_own), up_sum], axis=1)
    return produced.reshape(1, micro, tok, width), grads[None]


def solution(mesh):
    def run(*args):
        rows = args[7].shape[1] // mesh.shape["rep"]
        split = mesh.shape["section"] == 4 and mesh.shape["rep"] == 8 and rows % 128 == 0
        body = per_device if split else plain_device
        return jax.shard_map(
            body,
            mesh=mesh,
            in_specs=(
                P("section", "rep", None, None),
                P("section", "rep", None, None),
                P("section", "rep", None),
                P("rep", None),
                P("rep", None, None),
                P("section", None),
                P("section", None),
                P("section", "rep", None),
                P("section", "rep", None),
            ),
            out_specs=(P("section", "rep", None, None), P("section", "rep", None)),
            check_vma=False,
        )(*args)

    return run
```

```python
import functools

import jax
import jax.numpy as jnp
from jax import lax
from jax.experimental import pallas as pl
from jax.experimental.pallas import tpu as pltpu
from jax.sharding import PartitionSpec as P

EPSILON = 1e-05
HALF_ROOT = 0.7071067811865476
DENSITY = 0.3989422804014327


def from_behind(value, axis, steps):
    count = lax.axis_size(axis)
    leading, last = (max(0, -steps), min(count, count - steps))
    return lax.ppermute(value, axis, [(source, source + steps) for source in range(leading, last)])


def unpack_codes(levels):
    return levels.astype(jnp.float32)


def gelu_pair(preact):
    normal_cdf = 0.5 * (1.0 + lax.erf(preact * HALF_ROOT))
    bump = DENSITY * jnp.exp(-0.5 * preact * preact)
    return (preact * normal_cdf, normal_cdf + preact * bump)


def section_inputs(stored, packed, scaling, picks):
    chosen = jnp.take(stored, picks, axis=0).astype(jnp.float32)
    rebuilt = chosen + scaling[..., None] * unpack_codes(packed)
    return rebuilt.astype(jnp.bfloat16).reshape(-1, stored.shape[-1])


def normalize(inputs, gain_row, bias_row):
    values = inputs.astype(jnp.float32)
    centred = values - jnp.mean(values, axis=-1, keepdims=True)
    inv_std = lax.rsqrt(jnp.mean(centred * centred, axis=-1, keepdims=True) + EPSILON)
    scaled = centred * inv_std
    normed = (scaled * gain_row + bias_row).astype(jnp.bfloat16)
    return (normed, scaled, inv_std)


def input_grad(out_grad, back, gain_row, scaled, inv_std):
    weighted = back * gain_row
    inner = (
        weighted
        - jnp.mean(weighted, axis=-1, keepdims=True)
        - scaled * jnp.mean(weighted * scaled, axis=-1, keepdims=True)
    )
    return (out_grad.astype(jnp.float32) + inv_std * inner).astype(jnp.bfloat16)


def contract_rows(left, right):
    return lax.dot_general(
        left, right, (((0,), (0,)), ((), ())), preferred_element_type=jnp.float32
    )


def contract_cols(left, right):
    return lax.dot_general(
        left, right, (((1,), (1,)), ((), ())), preferred_element_type=jnp.float32
    )


def take_rows(source, begin, count):
    return lax.dynamic_slice_in_dim(source, begin, count, 0)


def put_rows(target, active, values, begin):
    older = lax.dynamic_slice_in_dim(target, begin, values.shape[0], 0)
    return lax.dynamic_update_slice_in_dim(target, jnp.where(active, values, older), begin, 0)


def plain_device(
    history, codes, scales, sample_ids, cotangent, ln_gain, ln_bias, down_weight, up_weight
):
    sections = lax.axis_size("section")
    position = lax.axis_index("section")
    w_down, w_up = (
        lax.all_gather(down_weight[0], "rep", axis=0, tiled=True),
        lax.all_gather(up_weight[0], "rep", axis=0, tiled=True),
    )
    inputs = section_inputs(history[0], codes[0], scales[0], sample_ids[0])
    gain_row = ln_gain[0]
    bias_row = ln_bias[0]
    normed, scaled, inv_std = normalize(inputs, gain_row, bias_row)
    activated, slopes = gelu_pair(jnp.dot(normed, w_down, preferred_element_type=jnp.float32))
    hidden = activated.astype(jnp.bfloat16)
    tok_count = cotangent.shape[1]
    row_total = inputs.shape[0]
    model_width = inputs.shape[1]
    rank_pair = 2 * w_down.shape[1]
    seeded = cotangent.reshape(row_total, model_width)
    pieces = 1
    block_size = tok_count // pieces
    blocks = row_total // block_size
    tick_count = blocks + sections - 1

    def advance(tick, carry):
        incoming, produced, running, kept_grad, kept_top = carry
        offset = tick - (sections - 1 - position)
        active = jnp.logical_and(offset >= 0, offset < blocks)
        begin = jnp.clip(offset, 0, blocks - 1) * block_size
        top_grad = take_rows(seeded, begin, block_size)
        out_grad = jnp.where(position == sections - 1, top_grad, incoming)
        slope_rows = take_rows(slopes, begin, block_size)
        scaled_rows = take_rows(scaled, begin, block_size)
        inv_rows = take_rows(inv_std, begin, block_size)
        act_grad = (
            jnp.dot(out_grad, w_up, preferred_element_type=jnp.float32) * slope_rows
        ).astype(jnp.bfloat16)
        back = contract_cols(act_grad, w_down)
        result = input_grad(out_grad, back, gain_row, scaled_rows, inv_rows)
        produced = put_rows(produced, active, result, begin)
        normed_rows = take_rows(normed, begin, block_size)
        hidden_rows = take_rows(hidden, begin, block_size)
        terms = jnp.concatenate(
            [contract_rows(normed_rows, act_grad), contract_rows(out_grad, hidden_rows)], axis=1
        )
        running = running + jnp.where(active, terms, 0.0)
        incoming = from_behind(result, "section", -1)
        return (incoming, produced, running, kept_grad, kept_top)

    start_in = jnp.zeros((block_size, model_width), jnp.bfloat16)
    start_out = jnp.zeros((row_total, model_width), jnp.bfloat16)
    start_sum = jnp.zeros((model_width, rank_pair), jnp.float32)
    start_grad = jnp.zeros((1, 1), jnp.bfloat16)
    start_top = jnp.zeros((1, 1), jnp.bfloat16)
    carry = lax.fori_loop(
        0, tick_count, advance, (start_in, start_out, start_sum, start_grad, start_top)
    )
    produced = carry[1]
    summed = lax.psum_scatter(
        (carry[2] / float(tok_count)).astype(jnp.bfloat16), "rep", scatter_dimension=0, tiled=True
    ).astype(jnp.float32)
    return (produced.reshape(1, row_total // tok_count, tok_count, model_width), summed[None])


VMEM_LIMIT = 16 * 1024 * 1024
F32 = jnp.float32
BF16 = jnp.bfloat16


def run_kernel(body, outs, args, grid=(1,), scalars=(), scratch=(), aliases=None, limit=VMEM_LIMIT):
    def whole(shape):
        return pl.BlockSpec(shape, lambda *_: (0,) * len(shape))

    arrays, in_specs, out_specs, out_shapes = [], [], [], []
    for arg in args:
        if isinstance(arg, tuple) and arg[1] is None:
            arrays.append(arg[0])
            in_specs.append(pl.BlockSpec(memory_space=pltpu.HBM))
        elif isinstance(arg, tuple):
            arrays.append(arg[0])
            in_specs.append(pl.BlockSpec(arg[1], arg[2]))
        else:
            arrays.append(arg)
            in_specs.append(whole(arg.shape))
    for out in outs:
        out_shapes.append(jax.ShapeDtypeStruct(out[0], out[1]))
        out_specs.append(pl.BlockSpec(out[2], out[3]) if len(out) > 2 else whole(out[0]))
    return pl.pallas_call(
        body,
        out_shape=out_shapes,
        grid_spec=pltpu.PrefetchScalarGridSpec(
            num_scalar_prefetch=len(scalars),
            grid=grid,
            in_specs=in_specs,
            out_specs=out_specs,
            scratch_shapes=list(scratch),
        ),
        input_output_aliases=aliases or {},
        compiler_params=pltpu.CompilerParams(vmem_limit_bytes=limit),
        cost_estimate=pl.CostEstimate(flops=0, bytes_accessed=0, transcendentals=0),
    )(*scalars, *arrays)


def regroup_body(
    blocks, picks, hist0, hist1, code0, code1, cot0, cot1, step, own, sent, stats, kept, *, micro, tok
):
    place = pl.program_id(0)
    last = pl.num_programs(0) - 1

    @pl.when(place < last)
    def _():
        for which, (hist, code, cot, out) in enumerate(
            ((hist0, code0, cot0, own), (hist1, code1, cot1, sent))
        ):
            for m in range(micro):
                rows = pl.ds(m * tok, tok)
                rebuilt = hist[picks[m]].astype(F32) + step[m] * code[m].astype(F32)
                rebuilt = rebuilt.astype(BF16)
                out[0, rows, :] = rebuilt
                out[1, rows, :] = cot[m]
                kept[2 * place + which, rows, :] = rebuilt

    @pl.when(place == last)
    def _():
        total, rows, lanes = kept.shape
        width = total * lanes

        def add(index, acc):
            return acc + jnp.sum(kept[index].astype(F32), axis=-1, keepdims=True)

        mean = lax.fori_loop(0, total, add, jnp.zeros((rows, 1), F32)) / width

        def add_square(index, acc):
            centred = kept[index].astype(F32) - mean
            return acc + jnp.sum(centred * centred, axis=-1, keepdims=True)

        var = lax.fori_loop(0, total, add_square, jnp.zeros((rows, 1), F32)) / width
        inv_std = lax.rsqrt(var + EPSILON)
        half = stats.shape[1] // 2
        stats[:, :half] = jnp.broadcast_to(mean, (rows, half))
        stats[:, half:] = jnp.broadcast_to(inv_std, (rows, half))
        lane = lax.broadcasted_iota(jnp.int32, (rows, 128), 1)
        packed = jnp.zeros((rows, 128), F32)
        for index, value in enumerate(bf16_parts(mean) + bf16_parts(inv_std)):
            packed = jnp.where(lane == index, value, packed)
        sent[0, :, :128] = packed.astype(BF16)


def bf16_parts(value):
    parts = []
    for _ in range(3):
        parts.append(value.astype(BF16).astype(F32))
        value = value - parts[-1]
    return parts


def split_stats(stats):
    if len(stats.shape) == 3:
        parts = stats[0].astype(F32)
        return [sum(parts[:, i : i + 1] for i in range(k, k + 3)) for k in (0, 3)]
    half = stats.shape[1] // 2
    return stats[:, 0:1], stats[:, half : half + 1]


def norm_body(blocks, own, sib, stats_own, stats_sib, gain, bias, out):
    tokens = own.shape[1]
    for slot, (values, stats) in enumerate(((own, stats_own), (sib, stats_sib))):
        mean, inv_std = split_stats(stats)
        scaled = (values[0].astype(F32) - mean) * inv_std
        out[slot * tokens : (slot + 1) * tokens, :] = (scaled * gain[...] + bias[...]).astype(BF16)


def as_column(row, lanes):
    turned = jnp.transpose(jnp.broadcast_to(row, (128, row.shape[1])))
    return jnp.concatenate([turned] * (lanes // 128), axis=1)


def step_body(*refs, first, sections):
    refs = refs[1:]
    own, sib, stats_own, stats_sib, gain, bias, down, up, near, far, diag_a, diag_b = refs[:12]
    refs = refs[12:]
    if first:
        old = None
        outs = refs
    else:
        old, outs = refs[:3], refs[3:]
    rank = down.shape[1]
    tokens = own.shape[1]
    weights = down[...]
    gain_row, bias_row = gain[...], bias[...]
    others = [near[...], far[...], jnp.concatenate([diag_a[...], diag_b[...]], axis=0)]
    for slot, (values, stats) in enumerate(((own, stats_own), (sib, stats_sib))):
        mean, inv_std = split_stats(stats)
        inputs = values[0]
        scaled = (inputs.astype(F32) - mean) * inv_std
        normed = (scaled * gain_row + bias_row).astype(BF16)
        pieces = [
            jnp.dot(values[1], up[...], preferred_element_type=F32),
            jnp.dot(normed, weights, preferred_element_type=F32),
        ] + [jnp.dot(inputs, other, preferred_element_type=F32) for other in others]
        for index, piece in enumerate(pieces):
            columns = slice(index * rank, (index + 1) * rank)
            if old is not None:
                piece = piece + old[slot][:, columns]
            outs[slot][:, columns] = piece
    wide = weights.astype(F32)
    gained = wide * as_column(gain_row, rank)
    biased = wide * as_column(bias_row, rank)
    gained_low = gained.astype(BF16)
    cross = outs[2]

    def put(rows, columns, value):
        if old is not None:
            value = value + old[2][rows, columns]
        cross[rows, columns] = value

    for index, other in enumerate(others):
        columns = slice(index * rank, (index + 1) * rank)
        put(slice(0, rank), columns, contract_rows(gained_low, other))
        put(
            slice(rank, rank + 1),
            columns,
            jnp.sum(other.astype(F32), axis=0, keepdims=True),
        )
    put(slice(rank + 1, rank + 2), slice(0, rank), jnp.sum(gained, axis=0, keepdims=True))
    put(slice(rank + 1, rank + 2), slice(rank, 2 * rank), jnp.sum(biased, axis=0, keepdims=True))


def chain_values(pre, slopes, centred, spread, cross, kappa, inv_std, width):
    act_grad = (pre * slopes).astype(BF16)
    wide = act_grad.astype(F32)
    second = jnp.sum(wide * centred, axis=-1, keepdims=True) / width
    return inv_std * (jnp.dot(act_grad, cross, preferred_element_type=F32) - second * spread)


def open_body(
    mine, got, cross, cross_got, stats, small, shared, spread_out, cross_out, kappa_out, near, rest, *, width
):
    rank = near.shape[1]
    total = mine[...] + got[...]
    both = cross[...] + cross_got[...]
    mean, inv_std = split_stats(stats)
    base = total[:, :rank]
    preact = total[:, rank : 2 * rank]
    sums = both[rank : rank + 1, :]
    kappa = both[rank + 1 : rank + 2, :rank]
    beta = both[rank + 1 : rank + 2, rank : 2 * rank]
    activated, slopes = gelu_pair(preact)
    centred = preact - beta
    spread = inv_std * (total[:, 2 * rank :] - mean * sums)
    kappa_column = as_column(kappa, rank)[:, 0:1]
    projected = (both[:rank, :] - kappa_column * (sums / width)).astype(BF16)
    small[:, :rank] = base
    small[:, rank:] = slopes
    shared[:, :rank] = activated
    shared[:, rank:] = centred
    spread_out[...] = spread
    cross_out[...] = projected
    kappa_out[...] = jnp.broadcast_to(kappa, kappa_out.shape)
    values = chain_values(base, slopes, centred, spread, projected, kappa, inv_std, width)
    near[...] = values[:, :rank].astype(BF16)
    rest[...] = values[:, rank:].astype(BF16)


def chain_body(*refs, width, turn):
    small, shared, spread, cross, kappa, stats = refs[:6]
    arrivals, out = refs[6:-1], refs[-1]
    rank = cross.shape[0]
    _, inv_std = split_stats(stats)
    pre = small[:, :rank]
    for arrival in arrivals:
        pre = pre + arrival[:, :rank].astype(F32)
    slopes = small[:, rank:]
    if turn == 3:
        out[...] = (pre * slopes).astype(BF16)
        return
    values = chain_values(
        pre, slopes, shared[:, rank:], spread[...], cross[...], kappa[0:1, :], inv_std, width
    )
    if turn == 1:
        out[:, :rank] = values[:, 2 * rank :].astype(BF16)
        out[:, rank:] = values[:, rank : 2 * rank].astype(BF16)
        return
    passed = arrivals[1][:, rank:].astype(F32) + arrivals[2][:, rank:].astype(F32)
    out[...] = (values[:, :rank] + passed).astype(BF16)


def grad_body(*refs, scale, width, index):
    *refs, held, sems = refs
    columns = pl.ds(index * held.shape[2], held.shape[2])
    copies = [
        pltpu.make_async_copy(source.at[0, :, columns], held.at[slot], sems.at[slot])
        for slot, source in enumerate(refs[1:3])
    ]
    for copy in copies:
        copy.start()
    stats_own, stats_sib, act_own, act_sib, shared_own, shared_sib, kappa = refs[3:10]
    gain, bias, down, term, *grads = refs[10:]
    gain_row, bias_row = gain[...], bias[...]
    weights = down[...]
    rank = weights.shape[1]
    total = None
    for slot, (stats, act, shared) in enumerate(
        ((stats_own, act_own, shared_own), (stats_sib, act_sib, shared_sib))
    ):
        mean, inv_std = split_stats(stats)
        act_grad = act[...]
        wide = act_grad.astype(F32)
        first = jnp.sum(wide * kappa[0:1, :], axis=-1, keepdims=True) / width
        second = jnp.sum(wide * shared[:, rank:], axis=-1, keepdims=True) / width
        copies[slot].wait()
        scaled = (held[slot].astype(F32) - mean) * inv_std
        normed = (scaled * gain_row + bias_row).astype(BF16)
        weighted = contract_cols(act_grad, weights) * gain_row
        tokens = act_grad.shape[0]
        term[slot * tokens : (slot + 1) * tokens, :] = (
            inv_std * (weighted - first - scaled * second)
        ).astype(BF16)
        piece = contract_rows(normed, act_grad)
        total = piece if total is None else total + piece
    for grad in grads:
        grad[...] = (total * scale).astype(BF16)


def ahead_body(normed, act, own, out, *, scale):
    out[...] = own[...].astype(F32) + contract_rows(normed[...], act[...]) * scale


def close_body(*refs, scale, count, index):
    *refs, held, sems = refs
    columns = pl.ds(index * held.shape[2], held.shape[2])
    copies = [
        pltpu.make_async_copy(source.at[1, :, columns], held.at[slot], sems.at[slot])
        for slot, source in enumerate(refs[1:3])
    ]
    for copy in copies:
        copy.start()
    level, _, _, shared_own, shared_sib, term = refs[0:6]
    arrivals = refs[6 : 6 + count]
    mine, theirs, grad = refs[6 + count :]
    rank = grad.shape[1]
    total = None
    for slot, (shared, out) in enumerate(((shared_own, mine), (shared_sib, theirs))):
        tokens = shared.shape[0]
        rows = slice(slot * tokens, (slot + 1) * tokens)
        copies[slot].wait()
        arrived = held[slot].astype(F32)
        for place, arrival in enumerate(arrivals):
            values = arrival[rows, :].astype(F32)
            if place == 0:
                values = jnp.where(level[0] % 2 == 0, values, 0.0)
            arrived = arrived + values
        out_grad = arrived.astype(BF16)
        out[...] = (out_grad.astype(F32) + term[rows, :].astype(F32)).astype(BF16)
        piece = contract_rows(out_grad, shared[:, :rank].astype(BF16))
        total = piece if total is None else total + piece
    grad[...] = (total * scale).astype(BF16)


def place_body(blocks, *refs, count):
    mines, arrived, out = refs[:count], refs[count], refs[-1]
    place = pl.program_id(0)
    for index, source in enumerate(mines):

        @pl.when(place == index)
        def _():
            out[...] = source[...]

    @pl.when(place >= count)
    def _():
        out[...] = arrived[...]


def per_device(
    history, codes, scales, sample_ids, cotangent, ln_gain, ln_bias, down_weight, up_weight
):
    sections = lax.axis_size("section")
    reps = lax.axis_size("rep")
    line = reps // 2
    section = lax.axis_index("section")
    rep = lax.axis_index("rep")
    chip, core = rep // 2, rep % 2
    _, micro, tok, width = history.shape
    tokens = micro * tok
    rows, rank = down_weight.shape[1:]

    def sibling(value):
        return lax.ppermute(value, "rep", [(r, r ^ 1) for r in range(reps)])

    def along(value, steps=1):
        return lax.ppermute(value, "rep", [(r, (r + 2 * steps) % reps) for r in range(reps)])

    def flip(value, mask):
        return lax.ppermute(value, "section", [(s, s ^ mask) for s in range(sections)])

    def after(value, *first):
        return lax.optimization_barrier((value, first))[0]

    chips = (chip - jnp.arange(line, dtype=jnp.int32)) % line
    blocks = jnp.concatenate([2 * chips + core, 2 * chips + 1 - core]).astype(jnp.int32)
    gain, bias = ln_gain, ln_bias

    ups, downs = [up_weight[0]], [down_weight[0]]
    cut = rows // 2

    def both(value):
        return flip(value, 1), flip(value, 2)

    def first_half(near, *first):
        return flip(after(near, *first)[:cut], 2)

    def second_half(far, *first):
        return flip(after(far, *first)[cut:], 1)

    nears = [both(ups[0])]
    ups.append(along(ups[0]))

    def columns(kind):
        return lambda i, blk, ids: (0, 0, blk[kind * line + jnp.minimum(i, line - 1)])

    own, sent, stats = run_kernel(
        functools.partial(regroup_body, micro=micro, tok=tok),
        [
            (
                (2, tokens, line * rows),
                BF16,
                (2, tokens, rows),
                lambda i, *_: (0, 0, jnp.minimum(i, line - 1)),
            ),
            ((2, tokens, (line + 1) * rows), BF16, (2, tokens, rows), lambda i, *_: (0, 0, i)),
            ((tokens, 256), F32),
        ],
        [
            (value, (micro, tok, rows), columns(kind))
            for value in (history[0], codes[0], cotangent)
            for kind in (0, 1)
        ]
        + [scales[0][..., None]],
        grid=(line + 1,),
        scalars=(blocks, sample_ids[0]),
        scratch=[pltpu.VMEM((2 * line, tokens, rows), BF16)],
    )
    sib = sibling(after(sent, *nears[0], ups[1]))
    stats_sib = (sib, (1, tokens, 128), lambda i, *_: (0, 0, line * rows // 128))

    ups.append(along(ups[1]))
    downs.append(along(after(downs[0], ups[1])))
    nears.append(both(ups[1]))
    def part(value, index):
        return (value, (2, tokens, rows), lambda i, *_: (0, 0, index))

    def one(value, kind, index):
        return (value, (1, tokens, rows), lambda i, *_: (kind, 0, index))

    def feature(value, index):
        return (value, (1, rows), lambda i, blk: (0, blk[index]))

    def add_step(sums, index, gathered):
        first = index == 0
        args = [
            part(own, index),
            part(sib, index),
            stats,
            stats_sib,
            feature(gain, index),
            feature(bias, index),
            downs[index],
            ups[index],
            *gathered,
        ]
        shapes = [
            ((tokens, (1 + sections) * rank), F32),
            ((tokens, (1 + sections) * rank), F32),
            ((rank + 8, (sections - 1) * rank), F32),
        ]
        return run_kernel(
            functools.partial(step_body, first=first, sections=sections),
            shapes,
            args + list(sums),
            scalars=(blocks,),
            aliases=None if first else {13 + i: i for i in range(3)},
            limit=28 * 1024 * 1024,
        )

    firsts = [first_half(nears[0][0], *nears[1])]
    ups.append(along(ups[2]))
    downs.append(along(downs[1]))
    nears.append(both(after(ups[2], *nears[1], sib)))
    seconds = [second_half(nears[0][1], *nears[2])]
    firsts.append(first_half(nears[1][0], *nears[2]))
    seconds.append(second_half(nears[1][1], *nears[2]))
    sums = add_step((), 0, nears[0] + (firsts[0], seconds[0]))
    nears.append(both(after(ups[3], *nears[2], *firsts, *seconds, *sums)))
    for index in range(2, line):
        firsts.append(first_half(nears[index][0]))
        seconds.append(second_half(nears[index][1]))
    (normed,) = run_kernel(
        norm_body,
        [((2 * tokens, rows), BF16)],
        [
            one(own, 0, 1),
            one(sib, 0, 1),
            stats,
            stats_sib,
            feature(gain, 1),
            feature(bias, 1),
        ],
        scalars=(blocks,),
    )
    downs.append(along(downs[2]))
    for index in range(1, line):
        sums = add_step(after(sums, normed), index, nears[index] + (firsts[index], seconds[index]))
    mine, other, cross = sums
    normed_ahead = along(after(normed, mine), -1)

    got, cross_got = sibling(other), sibling(cross)

    apart = sections - 1
    small, shared, spread, projected, kappa, to_next, to_rest = run_kernel(
        functools.partial(open_body, width=width),
        [
            ((tokens, 2 * rank), F32),
            ((tokens, 2 * rank), F32),
            ((tokens, apart * rank), F32),
            ((rank, apart * rank), BF16),
            ((8, rank), F32),
            ((tokens, rank), BF16),
            ((tokens, 2 * rank), BF16),
        ],
        [mine, got, cross, cross_got, stats],
    )
    arrivals = [lax.ppermute(to_next, "section", [(3, 2)])]
    late = lax.ppermute(to_rest, "section", [(3, 1)])
    state = [small, shared, spread, projected, kappa, stats]
    for turn in (1, 2, 3):
        (passed,) = run_kernel(
            functools.partial(chain_body, width=width, turn=turn),
            [((tokens, 2 * rank if turn == 1 else rank), BF16)],
            state + arrivals,
        )
        if turn == 1:
            arrivals += [late, lax.ppermute(passed, "section", [(2, 1)])]
        elif turn == 2:
            arrivals += [lax.ppermute(passed, "section", [(1, 0)])]
    act = passed
    act_sib, shared_sib = sibling(act), sibling(shared)

    scale = 1.0 / tok
    level = section.astype(jnp.int32).reshape(1)

    def grad_block(index, act):
        outs = [((2 * tokens, rows), BF16)]
        if index != 1:
            outs.append(((rows, rank), BF16))
        return run_kernel(
            functools.partial(grad_body, scale=scale, width=width, index=index),
            outs,
            [
                (own, None),
                (sib, None),
                stats,
                stats_sib,
                act,
                act_sib,
                shared,
                shared_sib,
                kappa,
                feature(gain, index),
                feature(bias, index),
                downs[index],
            ],
            scalars=(blocks,),
            scratch=[pltpu.VMEM((2, tokens, rows), BF16), pltpu.SemaphoreType.DMA((2,))],
        )

    def close_block(index, arrived):
        return run_kernel(
            functools.partial(close_body, scale=scale, count=len(arrived), index=index),
            [((tokens, rows), BF16), ((tokens, rows), BF16), ((rows, rank), BF16)],
            [(own, None), (sib, None), shared, shared_sib, terms[index], *arrived],
            scalars=(level,),
            scratch=[pltpu.VMEM((2, tokens, rows), BF16), pltpu.SemaphoreType.DMA((2,))],
        )

    terms, down_grads, up_grads, mines, theirs = {}, {}, {}, {}, {}
    act_sib = after(act_sib, normed_ahead)
    (terms[1],) = grad_block(1, act)
    act = after(act, terms[1])
    for index in (2, 3):
        terms[index], *down_grads[index] = grad_block(index, act)

    def add(*values):
        return sum(value.astype(F32) for value in values)

    def pass_on(running, part):
        return along(add(running, part).astype(BF16))

    def scan_open(index):
        return lax.ppermute(terms[index], "section", [(3, 2), (1, 0), (2, 3)])

    def scan_pairs(*pairs):
        return lax.ppermute(terms[1], "section", pairs)

    def scan_sum(index, arrived):
        return add(terms[index], arrived).astype(BF16)

    def scan_more(value):
        return lax.ppermute(value, "section", [(3, 1), (2, 0)])

    opened = {1: scan_pairs((3, 2), (2, 3))}
    beside = scan_pairs((1, 0))
    opened.update({index: scan_open(index) for index in (2, 3)})
    down_ring = along(down_grads[2][0])
    sums = {1: scan_sum(1, after(opened[1], terms[2], terms[3]))}
    more = {1: scan_more(sums[1])}
    down_sum = add(after(down_ring, beside), down_grads[3][0]).astype(BF16)
    down_ring = along(down_sum)
    sums[2] = scan_sum(2, after(opened[2], more[1]))
    more[2] = scan_more(sums[2])
    mines[1], theirs[1], up_grads[1] = close_block(
        1, (opened[1], after(more[1], down_sum, sums[2]), beside)
    )
    up_ring = along(up_grads[1])
    terms[0], *down_grads[0] = grad_block(0, after(act, up_grads[1]))
    opened[0] = scan_open(0)
    sums[3] = scan_sum(3, after(opened[3], sums[2]))
    more[3] = scan_more(sums[3])
    mines[2], theirs[2], up_grads[2] = close_block(
        2, (opened[2], after(more[2], sums[3], down_ring))
    )
    more[0] = scan_more(scan_sum(0, after(opened[0], sums[3], up_grads[2])))
    up_sum = add(up_ring, up_grads[2]).astype(BF16)
    up_ring = along(up_sum)
    act_ahead = along(jnp.concatenate(after([act, act_sib], up_sum), axis=0), -1)
    mines[3], theirs[3], up_grads[3] = close_block(3, (opened[3], after(more[3], act_ahead)))
    up_sum = add(up_ring, up_grads[3]).astype(BF16)
    up_ring = along(up_sum)
    def place(first, count, produced):
        sent = [theirs[index] for index in range(first, first + count)]
        arrived = sibling(jnp.concatenate(sent, axis=1) if count > 1 else sent[0])
        args = [mines[index] for index in range(first, first + count)]
        args.append((arrived, (tokens, rows), lambda i, blk: (0, jnp.maximum(i - count, 0))))
        if produced is not None:
            args.append((produced, None))

        def target(i, blk):
            return (0, blk[first + jnp.where(i < count, i, line + i - count)])

        return run_kernel(
            functools.partial(place_body, count=count),
            [((tokens, width), BF16, (tokens, rows), target)],
            args,
            grid=(2 * count,),
            scalars=(blocks,),
            aliases=None if produced is None else {len(args): 0},
        )[0]

    produced = place(1, line - 1, None)
    mines[0], theirs[0], up_grads[0] = close_block(
        0, (opened[0], after(more[0], up_ring, produced))
    )
    produced = place(0, 1, produced)
    (down_own,) = run_kernel(
        functools.partial(ahead_body, scale=scale),
        [((rows, rank), F32)],
        [normed_ahead, act_ahead, after(down_grads[0][0], mines[3])],
    )
    up_sum = add(up_ring, up_grads[0])
    grads = jnp.concatenate([add(down_ring, down_own), up_sum], axis=1)
    return produced.reshape(1, micro, tok, width), grads[None]


def solution(mesh):
    def run(*args):
        rows = args[7].shape[1] // mesh.shape["rep"]
        split = mesh.shape["section"] == 4 and mesh.shape["rep"] == 8 and rows % 128 == 0
        body = per_device if split else plain_device
        return jax.shard_map(
            body,
            mesh=mesh,
            in_specs=(
                P("section", "rep", None, None),
                P("section", "rep", None, None),
                P("section", "rep", None),
                P("rep", None),
                P("rep", None, None),
                P("section", None),
                P("section", None),
                P("section", "rep", None),
                P("section", "rep", None),
            ),
            out_specs=(P("section", "rep", None, None), P("section", "rep", None)),
            check_vma=False,
        )(*args)

    return run
```

```python
import functools

import jax
import jax.numpy as jnp
from jax import lax
from jax.experimental import pallas as pl
from jax.experimental.pallas import tpu as pltpu
from jax.sharding import PartitionSpec as P

EPSILON = 1e-05
HALF_ROOT = 0.7071067811865476
DENSITY = 0.3989422804014327


def from_behind(value, axis, steps):
    count = lax.axis_size(axis)
    leading, last = (max(0, -steps), min(count, count - steps))
    return lax.ppermute(value, axis, [(source, source + steps) for source in range(leading, last)])


def unpack_codes(levels):
    return levels.astype(jnp.float32)


def gelu_pair(preact):
    normal_cdf = 0.5 * (1.0 + lax.erf(preact * HALF_ROOT))
    bump = DENSITY * jnp.exp(-0.5 * preact * preact)
    return (preact * normal_cdf, normal_cdf + preact * bump)


def section_inputs(stored, packed, scaling, picks):
    chosen = jnp.take(stored, picks, axis=0).astype(jnp.float32)
    rebuilt = chosen + scaling[..., None] * unpack_codes(packed)
    return rebuilt.astype(jnp.bfloat16).reshape(-1, stored.shape[-1])


def normalize(inputs, gain_row, bias_row):
    values = inputs.astype(jnp.float32)
    centred = values - jnp.mean(values, axis=-1, keepdims=True)
    inv_std = lax.rsqrt(jnp.mean(centred * centred, axis=-1, keepdims=True) + EPSILON)
    scaled = centred * inv_std
    normed = (scaled * gain_row + bias_row).astype(jnp.bfloat16)
    return (normed, scaled, inv_std)


def input_grad(out_grad, back, gain_row, scaled, inv_std):
    weighted = back * gain_row
    inner = (
        weighted
        - jnp.mean(weighted, axis=-1, keepdims=True)
        - scaled * jnp.mean(weighted * scaled, axis=-1, keepdims=True)
    )
    return (out_grad.astype(jnp.float32) + inv_std * inner).astype(jnp.bfloat16)


def contract_rows(left, right):
    return lax.dot_general(
        left, right, (((0,), (0,)), ((), ())), preferred_element_type=jnp.float32
    )


def contract_cols(left, right):
    return lax.dot_general(
        left, right, (((1,), (1,)), ((), ())), preferred_element_type=jnp.float32
    )


def take_rows(source, begin, count):
    return lax.dynamic_slice_in_dim(source, begin, count, 0)


def put_rows(target, active, values, begin):
    older = lax.dynamic_slice_in_dim(target, begin, values.shape[0], 0)
    return lax.dynamic_update_slice_in_dim(target, jnp.where(active, values, older), begin, 0)


def plain_device(
    history, codes, scales, sample_ids, cotangent, ln_gain, ln_bias, down_weight, up_weight
):
    sections = lax.axis_size("section")
    position = lax.axis_index("section")
    w_down, w_up = (
        lax.all_gather(down_weight[0], "rep", axis=0, tiled=True),
        lax.all_gather(up_weight[0], "rep", axis=0, tiled=True),
    )
    inputs = section_inputs(history[0], codes[0], scales[0], sample_ids[0])
    gain_row = ln_gain[0]
    bias_row = ln_bias[0]
    normed, scaled, inv_std = normalize(inputs, gain_row, bias_row)
    activated, slopes = gelu_pair(jnp.dot(normed, w_down, preferred_element_type=jnp.float32))
    hidden = activated.astype(jnp.bfloat16)
    tok_count = cotangent.shape[1]
    row_total = inputs.shape[0]
    model_width = inputs.shape[1]
    rank_pair = 2 * w_down.shape[1]
    seeded = cotangent.reshape(row_total, model_width)
    pieces = 1
    block_size = tok_count // pieces
    blocks = row_total // block_size
    tick_count = blocks + sections - 1

    def advance(tick, carry):
        incoming, produced, running, kept_grad, kept_top = carry
        offset = tick - (sections - 1 - position)
        active = jnp.logical_and(offset >= 0, offset < blocks)
        begin = jnp.clip(offset, 0, blocks - 1) * block_size
        top_grad = take_rows(seeded, begin, block_size)
        out_grad = jnp.where(position == sections - 1, top_grad, incoming)
        slope_rows = take_rows(slopes, begin, block_size)
        scaled_rows = take_rows(scaled, begin, block_size)
        inv_rows = take_rows(inv_std, begin, block_size)
        act_grad = (
            jnp.dot(out_grad, w_up, preferred_element_type=jnp.float32) * slope_rows
        ).astype(jnp.bfloat16)
        back = contract_cols(act_grad, w_down)
        result = input_grad(out_grad, back, gain_row, scaled_rows, inv_rows)
        produced = put_rows(produced, active, result, begin)
        normed_rows = take_rows(normed, begin, block_size)
        hidden_rows = take_rows(hidden, begin, block_size)
        terms = jnp.concatenate(
            [contract_rows(normed_rows, act_grad), contract_rows(out_grad, hidden_rows)], axis=1
        )
        running = running + jnp.where(active, terms, 0.0)
        incoming = from_behind(result, "section", -1)
        return (incoming, produced, running, kept_grad, kept_top)

    start_in = jnp.zeros((block_size, model_width), jnp.bfloat16)
    start_out = jnp.zeros((row_total, model_width), jnp.bfloat16)
    start_sum = jnp.zeros((model_width, rank_pair), jnp.float32)
    start_grad = jnp.zeros((1, 1), jnp.bfloat16)
    start_top = jnp.zeros((1, 1), jnp.bfloat16)
    carry = lax.fori_loop(
        0, tick_count, advance, (start_in, start_out, start_sum, start_grad, start_top)
    )
    produced = carry[1]
    summed = lax.psum_scatter(
        (carry[2] / float(tok_count)).astype(jnp.bfloat16), "rep", scatter_dimension=0, tiled=True
    ).astype(jnp.float32)
    return (produced.reshape(1, row_total // tok_count, tok_count, model_width), summed[None])


VMEM_LIMIT = 16 * 1024 * 1024
F32 = jnp.float32
BF16 = jnp.bfloat16


def run_kernel(body, outs, args, grid=(1,), scalars=(), scratch=(), aliases=None, limit=VMEM_LIMIT):
    def whole(shape):
        return pl.BlockSpec(shape, lambda *_: (0,) * len(shape))

    arrays, in_specs, out_specs, out_shapes = [], [], [], []
    for arg in args:
        if isinstance(arg, tuple) and arg[1] is None:
            arrays.append(arg[0])
            in_specs.append(pl.BlockSpec(memory_space=pltpu.HBM))
        elif isinstance(arg, tuple):
            arrays.append(arg[0])
            in_specs.append(pl.BlockSpec(arg[1], arg[2]))
        else:
            arrays.append(arg)
            in_specs.append(whole(arg.shape))
    for out in outs:
        out_shapes.append(jax.ShapeDtypeStruct(out[0], out[1]))
        out_specs.append(pl.BlockSpec(out[2], out[3]) if len(out) > 2 else whole(out[0]))
    return pl.pallas_call(
        body,
        out_shape=out_shapes,
        grid_spec=pltpu.PrefetchScalarGridSpec(
            num_scalar_prefetch=len(scalars),
            grid=grid,
            in_specs=in_specs,
            out_specs=out_specs,
            scratch_shapes=list(scratch),
        ),
        input_output_aliases=aliases or {},
        compiler_params=pltpu.CompilerParams(vmem_limit_bytes=limit),
        cost_estimate=pl.CostEstimate(flops=0, bytes_accessed=0, transcendentals=0),
    )(*scalars, *arrays)


def regroup_body(
    blocks, picks, hist0, hist1, code0, code1, cot0, cot1, step, own, sent, stats, kept, *, micro, tok
):
    place = pl.program_id(0)
    last = pl.num_programs(0) - 1

    @pl.when(place < last)
    def _():
        for which, (hist, code, cot, out) in enumerate(
            ((hist0, code0, cot0, own), (hist1, code1, cot1, sent))
        ):
            for m in range(micro):
                rows = pl.ds(m * tok, tok)
                rebuilt = hist[picks[m]].astype(F32) + step[m] * code[m].astype(F32)
                rebuilt = rebuilt.astype(BF16)
                out[0, rows, :] = rebuilt
                out[1, rows, :] = cot[m]
                kept[2 * place + which, rows, :] = rebuilt

    @pl.when(place == last)
    def _():
        total, rows, lanes = kept.shape
        width = total * lanes

        def add(index, acc):
            return acc + jnp.sum(kept[index].astype(F32), axis=-1, keepdims=True)

        mean = lax.fori_loop(0, total, add, jnp.zeros((rows, 1), F32)) / width

        def add_square(index, acc):
            centred = kept[index].astype(F32) - mean
            return acc + jnp.sum(centred * centred, axis=-1, keepdims=True)

        var = lax.fori_loop(0, total, add_square, jnp.zeros((rows, 1), F32)) / width
        inv_std = lax.rsqrt(var + EPSILON)
        half = stats.shape[1] // 2
        stats[:, :half] = jnp.broadcast_to(mean, (rows, half))
        stats[:, half:] = jnp.broadcast_to(inv_std, (rows, half))
        lane = lax.broadcasted_iota(jnp.int32, (rows, 128), 1)
        packed = jnp.zeros((rows, 128), F32)
        for index, value in enumerate(bf16_parts(mean) + bf16_parts(inv_std)):
            packed = jnp.where(lane == index, value, packed)
        sent[0, :, :128] = packed.astype(BF16)


def bf16_parts(value):
    parts = []
    for _ in range(3):
        parts.append(value.astype(BF16).astype(F32))
        value = value - parts[-1]
    return parts


def split_stats(stats):
    if len(stats.shape) == 3:
        parts = stats[0].astype(F32)
        return [sum(parts[:, i : i + 1] for i in range(k, k + 3)) for k in (0, 3)]
    half = stats.shape[1] // 2
    return stats[:, 0:1], stats[:, half : half + 1]


def norm_body(blocks, own, sib, stats_own, stats_sib, gain, bias, out):
    tokens = own.shape[1]
    for slot, (values, stats) in enumerate(((own, stats_own), (sib, stats_sib))):
        mean, inv_std = split_stats(stats)
        scaled = (values[0].astype(F32) - mean) * inv_std
        out[slot * tokens : (slot + 1) * tokens, :] = (scaled * gain[...] + bias[...]).astype(BF16)


def as_column(row, lanes):
    turned = jnp.transpose(jnp.broadcast_to(row, (128, row.shape[1])))
    return jnp.concatenate([turned] * (lanes // 128), axis=1)


def step_body(*refs, first, sections):
    refs = refs[1:]
    own, sib, stats_own, stats_sib, gain, bias, down, up, near, far, diag_a, diag_b = refs[:12]
    refs = refs[12:]
    if first:
        old = None
        outs = refs
    else:
        old, outs = refs[:3], refs[3:]
    rank = down.shape[1]
    tokens = own.shape[1]
    weights = down[...]
    gain_row, bias_row = gain[...], bias[...]
    others = [near[...], far[...], jnp.concatenate([diag_a[...], diag_b[...]], axis=0)]
    for slot, (values, stats) in enumerate(((own, stats_own), (sib, stats_sib))):
        mean, inv_std = split_stats(stats)
        inputs = values[0]
        scaled = (inputs.astype(F32) - mean) * inv_std
        normed = (scaled * gain_row + bias_row).astype(BF16)
        pieces = [
            jnp.dot(values[1], up[...], preferred_element_type=F32),
            jnp.dot(normed, weights, preferred_element_type=F32),
        ] + [jnp.dot(inputs, other, preferred_element_type=F32) for other in others]
        for index, piece in enumerate(pieces):
            columns = slice(index * rank, (index + 1) * rank)
            if old is not None:
                piece = piece + old[slot][:, columns]
            outs[slot][:, columns] = piece
    wide = weights.astype(F32)
    gained = wide * as_column(gain_row, rank)
    biased = wide * as_column(bias_row, rank)
    gained_low = gained.astype(BF16)
    cross = outs[2]

    def put(rows, columns, value):
        if old is not None:
            value = value + old[2][rows, columns]
        cross[rows, columns] = value

    for index, other in enumerate(others):
        columns = slice(index * rank, (index + 1) * rank)
        put(slice(0, rank), columns, contract_rows(gained_low, other))
        put(
            slice(rank, rank + 1),
            columns,
            jnp.sum(other.astype(F32), axis=0, keepdims=True),
        )
    put(slice(rank + 1, rank + 2), slice(0, rank), jnp.sum(gained, axis=0, keepdims=True))
    put(slice(rank + 1, rank + 2), slice(rank, 2 * rank), jnp.sum(biased, axis=0, keepdims=True))


def chain_values(pre, slopes, centred, spread, cross, kappa, inv_std, width):
    act_grad = (pre * slopes).astype(BF16)
    wide = act_grad.astype(F32)
    second = jnp.sum(wide * centred, axis=-1, keepdims=True) / width
    return inv_std * (jnp.dot(act_grad, cross, preferred_element_type=F32) - second * spread)


def open_body(
    mine, got, cross, cross_got, stats, small, shared, spread_out, cross_out, kappa_out, near, rest, *, width
):
    rank = near.shape[1]
    total = mine[...] + got[...]
    both = cross[...] + cross_got[...]
    mean, inv_std = split_stats(stats)
    base = total[:, :rank]
    preact = total[:, rank : 2 * rank]
    sums = both[rank : rank + 1, :]
    kappa = both[rank + 1 : rank + 2, :rank]
    beta = both[rank + 1 : rank + 2, rank : 2 * rank]
    activated, slopes = gelu_pair(preact)
    centred = preact - beta
    spread = inv_std * (total[:, 2 * rank :] - mean * sums)
    kappa_column = as_column(kappa, rank)[:, 0:1]
    projected = (both[:rank, :] - kappa_column * (sums / width)).astype(BF16)
    small[:, :rank] = base
    small[:, rank:] = slopes
    shared[:, :rank] = activated
    shared[:, rank:] = centred
    spread_out[...] = spread
    cross_out[...] = projected
    kappa_out[...] = jnp.broadcast_to(kappa, kappa_out.shape)
    values = chain_values(base, slopes, centred, spread, projected, kappa, inv_std, width)
    near[...] = values[:, :rank].astype(BF16)
    rest[...] = values[:, rank:].astype(BF16)


def chain_body(*refs, width, turn):
    small, shared, spread, cross, kappa, stats = refs[:6]
    arrivals, out = refs[6:-1], refs[-1]
    rank = cross.shape[0]
    _, inv_std = split_stats(stats)
    pre = small[:, :rank]
    for arrival in arrivals:
        pre = pre + arrival[:, :rank].astype(F32)
    slopes = small[:, rank:]
    if turn == 3:
        out[...] = (pre * slopes).astype(BF16)
        return
    values = chain_values(
        pre, slopes, shared[:, rank:], spread[...], cross[...], kappa[0:1, :], inv_std, width
    )
    if turn == 1:
        out[:, :rank] = values[:, 2 * rank :].astype(BF16)
        out[:, rank:] = values[:, rank : 2 * rank].astype(BF16)
        return
    passed = arrivals[1][:, rank:].astype(F32) + arrivals[2][:, rank:].astype(F32)
    out[...] = (values[:, :rank] + passed).astype(BF16)


def grad_body(*refs, scale, width, index):
    *refs, held, sems = refs
    columns = pl.ds(index * held.shape[2], held.shape[2])
    copies = [
        pltpu.make_async_copy(source.at[0, :, columns], held.at[slot], sems.at[slot])
        for slot, source in enumerate(refs[1:3])
    ]
    for copy in copies:
        copy.start()
    stats_own, stats_sib, act_own, act_sib, shared_own, shared_sib, kappa = refs[3:10]
    gain, bias, down, term, *grads = refs[10:]
    gain_row, bias_row = gain[...], bias[...]
    weights = down[...]
    rank = weights.shape[1]
    total = None
    for slot, (stats, act, shared) in enumerate(
        ((stats_own, act_own, shared_own), (stats_sib, act_sib, shared_sib))
    ):
        mean, inv_std = split_stats(stats)
        act_grad = act[...]
        wide = act_grad.astype(F32)
        first = jnp.sum(wide * kappa[0:1, :], axis=-1, keepdims=True) / width
        second = jnp.sum(wide * shared[:, rank:], axis=-1, keepdims=True) / width
        copies[slot].wait()
        scaled = (held[slot].astype(F32) - mean) * inv_std
        normed = (scaled * gain_row + bias_row).astype(BF16)
        weighted = contract_cols(act_grad, weights) * gain_row
        tokens = act_grad.shape[0]
        term[slot * tokens : (slot + 1) * tokens, :] = (
            inv_std * (weighted - first - scaled * second)
        ).astype(BF16)
        piece = contract_rows(normed, act_grad)
        total = piece if total is None else total + piece
    for grad in grads:
        grad[...] = (total * scale).astype(BF16)


def ahead_body(normed, act, own, out, *, scale):
    out[...] = own[...].astype(F32) + contract_rows(normed[...], act[...]) * scale


def close_body(*refs, scale, count, index):
    *refs, held, sems = refs
    columns = pl.ds(index * held.shape[2], held.shape[2])
    copies = [
        pltpu.make_async_copy(source.at[1, :, columns], held.at[slot], sems.at[slot])
        for slot, source in enumerate(refs[1:3])
    ]
    for copy in copies:
        copy.start()
    level, _, _, shared_own, shared_sib, term = refs[0:6]
    arrivals = refs[6 : 6 + count]
    mine, theirs, grad = refs[6 + count :]
    rank = grad.shape[1]
    total = None
    for slot, (shared, out) in enumerate(((shared_own, mine), (shared_sib, theirs))):
        tokens = shared.shape[0]
        rows = slice(slot * tokens, (slot + 1) * tokens)
        copies[slot].wait()
        arrived = held[slot].astype(F32)
        for place, arrival in enumerate(arrivals):
            values = arrival[rows, :].astype(F32)
            if place == 0:
                values = jnp.where(level[0] % 2 == 0, values, 0.0)
            arrived = arrived + values
        out_grad = arrived.astype(BF16)
        out[...] = (out_grad.astype(F32) + term[rows, :].astype(F32)).astype(BF16)
        piece = contract_rows(out_grad, shared[:, :rank].astype(BF16))
        total = piece if total is None else total + piece
    grad[...] = (total * scale).astype(BF16)


def place_body(blocks, *refs, count):
    mines, arrived, out = refs[:count], refs[count], refs[-1]
    place = pl.program_id(0)
    for index, source in enumerate(mines):

        @pl.when(place == index)
        def _():
            out[...] = source[...]

    @pl.when(place >= count)
    def _():
        out[...] = arrived[...]


def per_device(
    history, codes, scales, sample_ids, cotangent, ln_gain, ln_bias, down_weight, up_weight
):
    sections = lax.axis_size("section")
    reps = lax.axis_size("rep")
    line = reps // 2
    section = lax.axis_index("section")
    rep = lax.axis_index("rep")
    chip, core = rep // 2, rep % 2
    _, micro, tok, width = history.shape
    tokens = micro * tok
    rows, rank = down_weight.shape[1:]

    def sibling(value):
        return lax.ppermute(value, "rep", [(r, r ^ 1) for r in range(reps)])

    def along(value, steps=1):
        return lax.ppermute(value, "rep", [(r, (r + 2 * steps) % reps) for r in range(reps)])

    def flip(value, mask):
        return lax.ppermute(value, "section", [(s, s ^ mask) for s in range(sections)])

    def after(value, *first):
        return lax.optimization_barrier((value, first))[0]

    chips = (chip - jnp.arange(line, dtype=jnp.int32)) % line
    blocks = jnp.concatenate([2 * chips + core, 2 * chips + 1 - core]).astype(jnp.int32)
    gain, bias = ln_gain, ln_bias

    ups, downs = [up_weight[0]], [down_weight[0]]
    cut = rows // 2

    def both(value):
        return flip(value, 1), flip(value, 2)

    def first_half(near, *first):
        return flip(after(near, *first)[:cut], 2)

    def second_half(far, *first):
        return flip(after(far, *first)[cut:], 1)

    nears = [both(ups[0])]
    ups.append(along(ups[0]))

    def columns(kind):
        return lambda i, blk, ids: (0, 0, blk[kind * line + jnp.minimum(i, line - 1)])

    own, sent, stats = run_kernel(
        functools.partial(regroup_body, micro=micro, tok=tok),
        [
            (
                (2, tokens, line * rows),
                BF16,
                (2, tokens, rows),
                lambda i, *_: (0, 0, jnp.minimum(i, line - 1)),
            ),
            ((2, tokens, (line + 1) * rows), BF16, (2, tokens, rows), lambda i, *_: (0, 0, i)),
            ((tokens, 256), F32),
        ],
        [
            (value, (micro, tok, rows), columns(kind))
            for value in (history[0], codes[0], cotangent)
            for kind in (0, 1)
        ]
        + [scales[0][..., None]],
        grid=(line + 1,),
        scalars=(blocks, sample_ids[0]),
        scratch=[pltpu.VMEM((2 * line, tokens, rows), BF16)],
    )
    sib = sibling(after(sent, *nears[0], ups[1]))
    stats_sib = (sib, (1, tokens, 128), lambda i, *_: (0, 0, line * rows // 128))

    ups.append(along(ups[1]))
    downs.append(along(after(downs[0], ups[1])))
    nears.append(both(ups[1]))
    def part(value, index):
        return (value, (2, tokens, rows), lambda i, *_: (0, 0, index))

    def one(value, kind, index):
        return (value, (1, tokens, rows), lambda i, *_: (kind, 0, index))

    def feature(value, index):
        return (value, (1, rows), lambda i, blk: (0, blk[index]))

    def add_step(sums, index, gathered):
        first = index == 0
        args = [
            part(own, index),
            part(sib, index),
            stats,
            stats_sib,
            feature(gain, index),
            feature(bias, index),
            downs[index],
            ups[index],
            *gathered,
        ]
        shapes = [
            ((tokens, (1 + sections) * rank), F32),
            ((tokens, (1 + sections) * rank), F32),
            ((rank + 8, (sections - 1) * rank), F32),
        ]
        return run_kernel(
            functools.partial(step_body, first=first, sections=sections),
            shapes,
            args + list(sums),
            scalars=(blocks,),
            aliases=None if first else {13 + i: i for i in range(3)},
            limit=28 * 1024 * 1024,
        )

    firsts = [first_half(nears[0][0], *nears[1])]
    ups.append(along(ups[2]))
    downs.append(along(downs[1]))
    nears.append(both(after(ups[2], *nears[1], sib)))
    seconds = [second_half(nears[0][1], *nears[2])]
    firsts.append(first_half(nears[1][0], *nears[2]))
    seconds.append(second_half(nears[1][1], *nears[2]))
    sums = add_step((), 0, nears[0] + (firsts[0], seconds[0]))
    nears.append(both(after(ups[3], *nears[2], *firsts, *seconds, *sums)))
    for index in range(2, line):
        firsts.append(first_half(nears[index][0]))
        seconds.append(second_half(nears[index][1]))
    (normed,) = run_kernel(
        norm_body,
        [((2 * tokens, rows), BF16)],
        [
            one(own, 0, 1),
            one(sib, 0, 1),
            stats,
            stats_sib,
            feature(gain, 1),
            feature(bias, 1),
        ],
        scalars=(blocks,),
    )
    downs.append(along(downs[2]))
    for index in range(1, line):
        sums = add_step(after(sums, normed), index, nears[index] + (firsts[index], seconds[index]))
    mine, other, cross = sums
    normed_ahead = along(after(normed, mine), -1)

    got, cross_got = sibling(other), sibling(cross)

    apart = sections - 1
    small, shared, spread, projected, kappa, to_next, to_rest = run_kernel(
        functools.partial(open_body, width=width),
        [
            ((tokens, 2 * rank), F32),
            ((tokens, 2 * rank), F32),
            ((tokens, apart * rank), F32),
            ((rank, apart * rank), BF16),
            ((8, rank), F32),
            ((tokens, rank), BF16),
            ((tokens, 2 * rank), BF16),
        ],
        [mine, got, cross, cross_got, stats],
    )
    arrivals = [lax.ppermute(to_next, "section", [(3, 2)])]
    late = lax.ppermute(to_rest, "section", [(3, 1)])
    state = [small, shared, spread, projected, kappa, stats]
    for turn in (1, 2, 3):
        (passed,) = run_kernel(
            functools.partial(chain_body, width=width, turn=turn),
            [((tokens, 2 * rank if turn == 1 else rank), BF16)],
            state + arrivals,
        )
        if turn == 1:
            arrivals += [late, lax.ppermute(passed, "section", [(2, 1)])]
        elif turn == 2:
            arrivals += [lax.ppermute(passed, "section", [(1, 0)])]
    act = passed
    act_sib, shared_sib = sibling(act), sibling(shared)

    scale = 1.0 / tok
    level = section.astype(jnp.int32).reshape(1)

    def grad_block(index, act):
        outs = [((2 * tokens, rows), BF16)]
        if index != 1:
            outs.append(((rows, rank), BF16))
        return run_kernel(
            functools.partial(grad_body, scale=scale, width=width, index=index),
            outs,
            [
                (own, None),
                (sib, None),
                stats,
                stats_sib,
                act,
                act_sib,
                shared,
                shared_sib,
                kappa,
                feature(gain, index),
                feature(bias, index),
                downs[index],
            ],
            scalars=(blocks,),
            scratch=[pltpu.VMEM((2, tokens, rows), BF16), pltpu.SemaphoreType.DMA((2,))],
        )

    def close_block(index, arrived):
        return run_kernel(
            functools.partial(close_body, scale=scale, count=len(arrived), index=index),
            [((tokens, rows), BF16), ((tokens, rows), BF16), ((rows, rank), BF16)],
            [(own, None), (sib, None), shared, shared_sib, terms[index], *arrived],
            scalars=(level,),
            scratch=[pltpu.VMEM((2, tokens, rows), BF16), pltpu.SemaphoreType.DMA((2,))],
        )

    terms, down_grads, up_grads, mines, theirs = {}, {}, {}, {}, {}
    act_sib = after(act_sib, normed_ahead)
    (terms[1],) = grad_block(1, act)
    act = after(act, terms[1])
    act_ahead = along(jnp.concatenate([act, act_sib], axis=0), -1)
    terms[2], *down_grads[2] = grad_block(2, act)
    terms[3], *down_grads[3] = grad_block(3, after(act, act_ahead))

    def add(*values):
        return sum(value.astype(F32) for value in values)

    def pass_on(running, part):
        return along(add(running, part).astype(BF16))

    def scan_open(index):
        return lax.ppermute(terms[index], "section", [(3, 2), (1, 0), (2, 3)])

    def scan_pairs(*pairs):
        return lax.ppermute(terms[1], "section", pairs)

    def scan_sum(index, arrived):
        return add(terms[index], arrived).astype(BF16)

    def scan_more(value):
        return lax.ppermute(value, "section", [(3, 1), (2, 0)])

    opened = {1: scan_pairs((3, 2), (2, 3))}
    beside = scan_pairs((1, 0))
    opened.update({index: scan_open(index) for index in (2, 3)})
    down_ring = along(down_grads[2][0])
    sums = {1: scan_sum(1, after(opened[1], terms[2], terms[3]))}
    more = {1: scan_more(sums[1])}
    down_sum = add(after(down_ring, beside), down_grads[3][0]).astype(BF16)
    down_ring = along(down_sum)
    sums[2] = scan_sum(2, after(opened[2], more[1]))
    more[2] = scan_more(sums[2])
    mines[1], theirs[1], up_grads[1] = close_block(
        1, (opened[1], after(more[1], down_sum, sums[2]), beside)
    )
    up_ring = along(up_grads[1])
    terms[0], *down_grads[0] = grad_block(0, after(act, up_grads[1]))
    opened[0] = scan_open(0)
    sums[3] = scan_sum(3, after(opened[3], sums[2], up_grads[1]))
    more[3] = scan_more(sums[3])
    mines[2], theirs[2], up_grads[2] = close_block(
        2, (opened[2], after(more[2], sums[3], down_ring))
    )
    more[0] = scan_more(scan_sum(0, after(opened[0], sums[3], up_grads[2])))
    halves = [slice(0, rows // 2), slice(rows // 2, rows)]
    up_sums = [add(up_ring[half], up_grads[2][half]).astype(BF16) for half in halves]
    up_ring = [along(value) for value in up_sums]
    mines[3], theirs[3], up_grads[3] = close_block(3, (opened[3], after(more[3], *up_sums)))
    up_sums = [add(up_ring[0], up_grads[3][halves[0]]).astype(BF16)]
    second = after(up_ring[1], up_sums[0])
    up_sums.append(add(second, up_grads[3][halves[1]]).astype(BF16))
    up_ring = [along(value) for value in up_sums]

    def place(first, count, produced):
        sent = [theirs[index] for index in range(first, first + count)]
        arrived = sibling(jnp.concatenate(sent, axis=1) if count > 1 else sent[0])
        args = [mines[index] for index in range(first, first + count)]
        args.append((arrived, (tokens, rows), lambda i, blk: (0, jnp.maximum(i - count, 0))))
        if produced is not None:
            args.append((produced, None))

        def target(i, blk):
            return (0, blk[first + jnp.where(i < count, i, line + i - count)])

        return run_kernel(
            functools.partial(place_body, count=count),
            [((tokens, width), BF16, (tokens, rows), target)],
            args,
            grid=(2 * count,),
            scalars=(blocks,),
            aliases=None if produced is None else {len(args): 0},
        )[0]

    produced = place(1, line - 1, None)
    mines[0], theirs[0], up_grads[0] = close_block(
        0, (opened[0], after(more[0], up_ring[0], up_sums[1], produced))
    )
    produced = place(0, 1, produced)
    (down_own,) = run_kernel(
        functools.partial(ahead_body, scale=scale),
        [((rows, rank), F32)],
        [normed_ahead, act_ahead, after(down_grads[0][0], mines[3])],
    )
    up_sum = add(jnp.concatenate(up_ring, axis=0), up_grads[0])
    grads = jnp.concatenate([add(down_ring, down_own), up_sum], axis=1)
    return produced.reshape(1, micro, tok, width), grads[None]


def solution(mesh):
    def run(*args):
        rows = args[7].shape[1] // mesh.shape["rep"]
        split = mesh.shape["section"] == 4 and mesh.shape["rep"] == 8 and rows % 128 == 0
        body = per_device if split else plain_device
        return jax.shard_map(
            body,
            mesh=mesh,
            in_specs=(
                P("section", "rep", None, None),
                P("section", "rep", None, None),
                P("section", "rep", None),
                P("rep", None),
                P("rep", None, None),
                P("section", None),
                P("section", None),
                P("section", "rep", None),
                P("section", "rep", None),
            ),
            out_specs=(P("section", "rep", None, None), P("section", "rep", None)),
            check_vma=False,
        )(*args)

    return run
```

```python
import functools

import jax
import jax.numpy as jnp
from jax import lax
from jax.experimental import pallas as pl
from jax.experimental.pallas import tpu as pltpu
from jax.sharding import PartitionSpec as P

EPSILON = 1e-05
HALF_ROOT = 0.7071067811865476
DENSITY = 0.3989422804014327


def from_behind(value, axis, steps):
    count = lax.axis_size(axis)
    leading, last = (max(0, -steps), min(count, count - steps))
    return lax.ppermute(value, axis, [(source, source + steps) for source in range(leading, last)])


def unpack_codes(levels):
    return levels.astype(jnp.float32)


def gelu_pair(preact):
    normal_cdf = 0.5 * (1.0 + lax.erf(preact * HALF_ROOT))
    bump = DENSITY * jnp.exp(-0.5 * preact * preact)
    return (preact * normal_cdf, normal_cdf + preact * bump)


def section_inputs(stored, packed, scaling, picks):
    chosen = jnp.take(stored, picks, axis=0).astype(jnp.float32)
    rebuilt = chosen + scaling[..., None] * unpack_codes(packed)
    return rebuilt.astype(jnp.bfloat16).reshape(-1, stored.shape[-1])


def normalize(inputs, gain_row, bias_row):
    values = inputs.astype(jnp.float32)
    centred = values - jnp.mean(values, axis=-1, keepdims=True)
    inv_std = lax.rsqrt(jnp.mean(centred * centred, axis=-1, keepdims=True) + EPSILON)
    scaled = centred * inv_std
    normed = (scaled * gain_row + bias_row).astype(jnp.bfloat16)
    return (normed, scaled, inv_std)


def input_grad(out_grad, back, gain_row, scaled, inv_std):
    weighted = back * gain_row
    inner = (
        weighted
        - jnp.mean(weighted, axis=-1, keepdims=True)
        - scaled * jnp.mean(weighted * scaled, axis=-1, keepdims=True)
    )
    return (out_grad.astype(jnp.float32) + inv_std * inner).astype(jnp.bfloat16)


def contract_rows(left, right):
    return lax.dot_general(
        left, right, (((0,), (0,)), ((), ())), preferred_element_type=jnp.float32
    )


def contract_cols(left, right):
    return lax.dot_general(
        left, right, (((1,), (1,)), ((), ())), preferred_element_type=jnp.float32
    )


def take_rows(source, begin, count):
    return lax.dynamic_slice_in_dim(source, begin, count, 0)


def put_rows(target, active, values, begin):
    older = lax.dynamic_slice_in_dim(target, begin, values.shape[0], 0)
    return lax.dynamic_update_slice_in_dim(target, jnp.where(active, values, older), begin, 0)


def plain_device(
    history, codes, scales, sample_ids, cotangent, ln_gain, ln_bias, down_weight, up_weight
):
    sections = lax.axis_size("section")
    position = lax.axis_index("section")
    w_down, w_up = (
        lax.all_gather(down_weight[0], "rep", axis=0, tiled=True),
        lax.all_gather(up_weight[0], "rep", axis=0, tiled=True),
    )
    inputs = section_inputs(history[0], codes[0], scales[0], sample_ids[0])
    gain_row = ln_gain[0]
    bias_row = ln_bias[0]
    normed, scaled, inv_std = normalize(inputs, gain_row, bias_row)
    activated, slopes = gelu_pair(jnp.dot(normed, w_down, preferred_element_type=jnp.float32))
    hidden = activated.astype(jnp.bfloat16)
    tok_count = cotangent.shape[1]
    row_total = inputs.shape[0]
    model_width = inputs.shape[1]
    rank_pair = 2 * w_down.shape[1]
    seeded = cotangent.reshape(row_total, model_width)
    pieces = 1
    block_size = tok_count // pieces
    blocks = row_total // block_size
    tick_count = blocks + sections - 1

    def advance(tick, carry):
        incoming, produced, running, kept_grad, kept_top = carry
        offset = tick - (sections - 1 - position)
        active = jnp.logical_and(offset >= 0, offset < blocks)
        begin = jnp.clip(offset, 0, blocks - 1) * block_size
        top_grad = take_rows(seeded, begin, block_size)
        out_grad = jnp.where(position == sections - 1, top_grad, incoming)
        slope_rows = take_rows(slopes, begin, block_size)
        scaled_rows = take_rows(scaled, begin, block_size)
        inv_rows = take_rows(inv_std, begin, block_size)
        act_grad = (
            jnp.dot(out_grad, w_up, preferred_element_type=jnp.float32) * slope_rows
        ).astype(jnp.bfloat16)
        back = contract_cols(act_grad, w_down)
        result = input_grad(out_grad, back, gain_row, scaled_rows, inv_rows)
        produced = put_rows(produced, active, result, begin)
        normed_rows = take_rows(normed, begin, block_size)
        hidden_rows = take_rows(hidden, begin, block_size)
        terms = jnp.concatenate(
            [contract_rows(normed_rows, act_grad), contract_rows(out_grad, hidden_rows)], axis=1
        )
        running = running + jnp.where(active, terms, 0.0)
        incoming = from_behind(result, "section", -1)
        return (incoming, produced, running, kept_grad, kept_top)

    start_in = jnp.zeros((block_size, model_width), jnp.bfloat16)
    start_out = jnp.zeros((row_total, model_width), jnp.bfloat16)
    start_sum = jnp.zeros((model_width, rank_pair), jnp.float32)
    start_grad = jnp.zeros((1, 1), jnp.bfloat16)
    start_top = jnp.zeros((1, 1), jnp.bfloat16)
    carry = lax.fori_loop(
        0, tick_count, advance, (start_in, start_out, start_sum, start_grad, start_top)
    )
    produced = carry[1]
    summed = lax.psum_scatter(
        (carry[2] / float(tok_count)).astype(jnp.bfloat16), "rep", scatter_dimension=0, tiled=True
    ).astype(jnp.float32)
    return (produced.reshape(1, row_total // tok_count, tok_count, model_width), summed[None])


VMEM_LIMIT = 16 * 1024 * 1024
F32 = jnp.float32
BF16 = jnp.bfloat16


def run_kernel(body, outs, args, grid=(1,), scalars=(), scratch=(), aliases=None, limit=VMEM_LIMIT):
    def whole(shape):
        return pl.BlockSpec(shape, lambda *_: (0,) * len(shape))

    arrays, in_specs, out_specs, out_shapes = [], [], [], []
    for arg in args:
        if isinstance(arg, tuple) and arg[1] is None:
            arrays.append(arg[0])
            in_specs.append(pl.BlockSpec(memory_space=pltpu.HBM))
        elif isinstance(arg, tuple):
            arrays.append(arg[0])
            in_specs.append(pl.BlockSpec(arg[1], arg[2]))
        else:
            arrays.append(arg)
            in_specs.append(whole(arg.shape))
    for out in outs:
        out_shapes.append(jax.ShapeDtypeStruct(out[0], out[1]))
        out_specs.append(pl.BlockSpec(out[2], out[3]) if len(out) > 2 else whole(out[0]))
    return pl.pallas_call(
        body,
        out_shape=out_shapes,
        grid_spec=pltpu.PrefetchScalarGridSpec(
            num_scalar_prefetch=len(scalars),
            grid=grid,
            in_specs=in_specs,
            out_specs=out_specs,
            scratch_shapes=list(scratch),
        ),
        input_output_aliases=aliases or {},
        compiler_params=pltpu.CompilerParams(vmem_limit_bytes=limit),
        cost_estimate=pl.CostEstimate(flops=0, bytes_accessed=0, transcendentals=0),
    )(*scalars, *arrays)


def regroup_body(
    blocks, picks, hist0, hist1, code0, code1, cot0, cot1, step, own, sent, stats, kept, *, micro, tok
):
    place = pl.program_id(0)
    last = pl.num_programs(0) - 1

    @pl.when(place < last)
    def _():
        for which, (hist, code, cot, out) in enumerate(
            ((hist0, code0, cot0, own), (hist1, code1, cot1, sent))
        ):
            for m in range(micro):
                rows = pl.ds(m * tok, tok)
                rebuilt = hist[picks[m]].astype(F32) + step[m] * code[m].astype(F32)
                rebuilt = rebuilt.astype(BF16)
                out[0, rows, :] = rebuilt
                out[1, rows, :] = cot[m]
                kept[2 * place + which, rows, :] = rebuilt

    @pl.when(place == last)
    def _():
        total, rows, lanes = kept.shape
        width = total * lanes

        def add(index, acc):
            return acc + jnp.sum(kept[index].astype(F32), axis=-1, keepdims=True)

        mean = lax.fori_loop(0, total, add, jnp.zeros((rows, 1), F32)) / width

        def add_square(index, acc):
            centred = kept[index].astype(F32) - mean
            return acc + jnp.sum(centred * centred, axis=-1, keepdims=True)

        var = lax.fori_loop(0, total, add_square, jnp.zeros((rows, 1), F32)) / width
        inv_std = lax.rsqrt(var + EPSILON)
        half = stats.shape[1] // 2
        stats[:, :half] = jnp.broadcast_to(mean, (rows, half))
        stats[:, half:] = jnp.broadcast_to(inv_std, (rows, half))
        lane = lax.broadcasted_iota(jnp.int32, (rows, 128), 1)
        packed = jnp.zeros((rows, 128), F32)
        for index, value in enumerate(bf16_parts(mean) + bf16_parts(inv_std)):
            packed = jnp.where(lane == index, value, packed)
        sent[0, :, :128] = packed.astype(BF16)


def bf16_parts(value):
    parts = []
    for _ in range(3):
        parts.append(value.astype(BF16).astype(F32))
        value = value - parts[-1]
    return parts


def split_stats(stats):
    if len(stats.shape) == 3:
        parts = stats[0].astype(F32)
        return [sum(parts[:, i : i + 1] for i in range(k, k + 3)) for k in (0, 3)]
    half = stats.shape[1] // 2
    return stats[:, 0:1], stats[:, half : half + 1]


def norm_body(blocks, own, sib, stats_own, stats_sib, gain, bias, out):
    tokens = own.shape[1]
    for slot, (values, stats) in enumerate(((own, stats_own), (sib, stats_sib))):
        mean, inv_std = split_stats(stats)
        scaled = (values[0].astype(F32) - mean) * inv_std
        out[slot * tokens : (slot + 1) * tokens, :] = (scaled * gain[...] + bias[...]).astype(BF16)


def as_column(row, lanes):
    turned = jnp.transpose(jnp.broadcast_to(row, (128, row.shape[1])))
    return jnp.concatenate([turned] * (lanes // 128), axis=1)


def step_body(*refs, first, sections):
    refs = refs[1:]
    own, sib, stats_own, stats_sib, gain, bias, down, up, near, far, diag_a, diag_b = refs[:12]
    refs = refs[12:]
    if first:
        old = None
        outs = refs
    else:
        old, outs = refs[:3], refs[3:]
    rank = down.shape[1]
    tokens = own.shape[1]
    weights = down[...]
    gain_row, bias_row = gain[...], bias[...]
    others = [near[...], far[...], jnp.concatenate([diag_a[...], diag_b[...]], axis=0)]
    for slot, (values, stats) in enumerate(((own, stats_own), (sib, stats_sib))):
        mean, inv_std = split_stats(stats)
        inputs = values[0]
        scaled = (inputs.astype(F32) - mean) * inv_std
        normed = (scaled * gain_row + bias_row).astype(BF16)
        pieces = [
            jnp.dot(values[1], up[...], preferred_element_type=F32),
            jnp.dot(normed, weights, preferred_element_type=F32),
        ] + [jnp.dot(inputs, other, preferred_element_type=F32) for other in others]
        for index, piece in enumerate(pieces):
            columns = slice(index * rank, (index + 1) * rank)
            if old is not None:
                piece = piece + old[slot][:, columns]
            outs[slot][:, columns] = piece
    wide = weights.astype(F32)
    gained = wide * as_column(gain_row, rank)
    biased = wide * as_column(bias_row, rank)
    gained_low = gained.astype(BF16)
    cross = outs[2]

    def put(rows, columns, value):
        if old is not None:
            value = value + old[2][rows, columns]
        cross[rows, columns] = value

    for index, other in enumerate(others):
        columns = slice(index * rank, (index + 1) * rank)
        put(slice(0, rank), columns, contract_rows(gained_low, other))
        put(
            slice(rank, rank + 1),
            columns,
            jnp.sum(other.astype(F32), axis=0, keepdims=True),
        )
    put(slice(rank + 1, rank + 2), slice(0, rank), jnp.sum(gained, axis=0, keepdims=True))
    put(slice(rank + 1, rank + 2), slice(rank, 2 * rank), jnp.sum(biased, axis=0, keepdims=True))


def chain_values(pre, slopes, centred, spread, cross, kappa, inv_std, width):
    act_grad = (pre * slopes).astype(BF16)
    wide = act_grad.astype(F32)
    second = jnp.sum(wide * centred, axis=-1, keepdims=True) / width
    return inv_std * (jnp.dot(act_grad, cross, preferred_element_type=F32) - second * spread)


def open_body(
    mine, got, cross, cross_got, stats, small, shared, spread_out, cross_out, kappa_out, near, rest, *, width
):
    rank = near.shape[1]
    total = mine[...] + got[...]
    both = cross[...] + cross_got[...]
    mean, inv_std = split_stats(stats)
    base = total[:, :rank]
    preact = total[:, rank : 2 * rank]
    sums = both[rank : rank + 1, :]
    kappa = both[rank + 1 : rank + 2, :rank]
    beta = both[rank + 1 : rank + 2, rank : 2 * rank]
    activated, slopes = gelu_pair(preact)
    centred = preact - beta
    spread = inv_std * (total[:, 2 * rank :] - mean * sums)
    kappa_column = as_column(kappa, rank)[:, 0:1]
    projected = (both[:rank, :] - kappa_column * (sums / width)).astype(BF16)
    small[:, :rank] = base
    small[:, rank:] = slopes
    shared[:, :rank] = activated
    shared[:, rank:] = centred
    spread_out[...] = spread
    cross_out[...] = projected
    kappa_out[...] = jnp.broadcast_to(kappa, kappa_out.shape)
    values = chain_values(base, slopes, centred, spread, projected, kappa, inv_std, width)
    near[...] = values[:, :rank].astype(BF16)
    rest[...] = values[:, rank:].astype(BF16)


def chain_body(*refs, width, turn):
    small, shared, spread, cross, kappa, stats = refs[:6]
    arrivals, out = refs[6:-1], refs[-1]
    rank = cross.shape[0]
    _, inv_std = split_stats(stats)
    pre = small[:, :rank]
    for arrival in arrivals:
        pre = pre + arrival[:, :rank].astype(F32)
    slopes = small[:, rank:]
    if turn == 3:
        out[...] = (pre * slopes).astype(BF16)
        return
    values = chain_values(
        pre, slopes, shared[:, rank:], spread[...], cross[...], kappa[0:1, :], inv_std, width
    )
    if turn == 1:
        out[:, :rank] = values[:, 2 * rank :].astype(BF16)
        out[:, rank:] = values[:, rank : 2 * rank].astype(BF16)
        return
    passed = arrivals[1][:, rank:].astype(F32) + arrivals[2][:, rank:].astype(F32)
    out[...] = (values[:, :rank] + passed).astype(BF16)


def grad_body(*refs, scale, width, index):
    *refs, held, sems = refs
    columns = pl.ds(index * held.shape[2], held.shape[2])
    copies = [
        pltpu.make_async_copy(source.at[0, :, columns], held.at[slot], sems.at[slot])
        for slot, source in enumerate(refs[1:3])
    ]
    for copy in copies:
        copy.start()
    stats_own, stats_sib, act_own, act_sib, shared_own, shared_sib, kappa = refs[3:10]
    gain, bias, down, term, *grads = refs[10:]
    gain_row, bias_row = gain[...], bias[...]
    weights = down[...]
    rank = weights.shape[1]
    total = None
    for slot, (stats, act, shared) in enumerate(
        ((stats_own, act_own, shared_own), (stats_sib, act_sib, shared_sib))
    ):
        mean, inv_std = split_stats(stats)
        act_grad = act[...]
        wide = act_grad.astype(F32)
        first = jnp.sum(wide * kappa[0:1, :], axis=-1, keepdims=True) / width
        second = jnp.sum(wide * shared[:, rank:], axis=-1, keepdims=True) / width
        copies[slot].wait()
        scaled = (held[slot].astype(F32) - mean) * inv_std
        normed = (scaled * gain_row + bias_row).astype(BF16)
        weighted = contract_cols(act_grad, weights) * gain_row
        tokens = act_grad.shape[0]
        term[slot * tokens : (slot + 1) * tokens, :] = (
            inv_std * (weighted - first - scaled * second)
        ).astype(BF16)
        piece = contract_rows(normed, act_grad)
        total = piece if total is None else total + piece
    for grad in grads:
        grad[...] = (total * scale).astype(BF16)


def ahead_body(normed, act, own, out, *, scale):
    out[...] = own[...].astype(F32) + contract_rows(normed[...], act[...]) * scale


def close_body(*refs, scale, count, index):
    *refs, held, sems = refs
    columns = pl.ds(index * held.shape[2], held.shape[2])
    copies = [
        pltpu.make_async_copy(source.at[1, :, columns], held.at[slot], sems.at[slot])
        for slot, source in enumerate(refs[1:3])
    ]
    for copy in copies:
        copy.start()
    level, _, _, shared_own, shared_sib, term = refs[0:6]
    arrivals = refs[6 : 6 + count]
    mine, theirs, grad = refs[6 + count :]
    rank = grad.shape[1]
    total = None
    for slot, (shared, out) in enumerate(((shared_own, mine), (shared_sib, theirs))):
        tokens = shared.shape[0]
        rows = slice(slot * tokens, (slot + 1) * tokens)
        copies[slot].wait()
        arrived = held[slot].astype(F32)
        for place, arrival in enumerate(arrivals):
            values = arrival[rows, :].astype(F32)
            if place == 0:
                values = jnp.where(level[0] % 2 == 0, values, 0.0)
            arrived = arrived + values
        out_grad = arrived.astype(BF16)
        out[...] = (out_grad.astype(F32) + term[rows, :].astype(F32)).astype(BF16)
        piece = contract_rows(out_grad, shared[:, :rank].astype(BF16))
        total = piece if total is None else total + piece
    grad[...] = (total * scale).astype(BF16)


def place_body(blocks, *refs, count):
    mines, arrived, out = refs[:count], refs[count], refs[-1]
    place = pl.program_id(0)
    for index, source in enumerate(mines):

        @pl.when(place == index)
        def _():
            out[...] = source[...]

    @pl.when(place >= count)
    def _():
        out[...] = arrived[...]


def per_device(
    history, codes, scales, sample_ids, cotangent, ln_gain, ln_bias, down_weight, up_weight
):
    sections = lax.axis_size("section")
    reps = lax.axis_size("rep")
    line = reps // 2
    section = lax.axis_index("section")
    rep = lax.axis_index("rep")
    chip, core = rep // 2, rep % 2
    _, micro, tok, width = history.shape
    tokens = micro * tok
    rows, rank = down_weight.shape[1:]

    def sibling(value):
        return lax.ppermute(value, "rep", [(r, r ^ 1) for r in range(reps)])

    def along(value, steps=1):
        return lax.ppermute(value, "rep", [(r, (r + 2 * steps) % reps) for r in range(reps)])

    def flip(value, mask):
        return lax.ppermute(value, "section", [(s, s ^ mask) for s in range(sections)])

    def after(value, *first):
        return lax.optimization_barrier((value, first))[0]

    chips = (chip - jnp.arange(line, dtype=jnp.int32)) % line
    blocks = jnp.concatenate([2 * chips + core, 2 * chips + 1 - core]).astype(jnp.int32)
    gain, bias = ln_gain, ln_bias

    ups, downs = [up_weight[0]], [down_weight[0]]
    cut = rows // 2

    def both(value):
        return flip(value, 1), flip(value, 2)

    def first_half(near, *first):
        return flip(after(near, *first)[:cut], 2)

    def second_half(far, *first):
        return flip(after(far, *first)[cut:], 1)

    nears = [both(ups[0])]
    ups.append(along(ups[0]))

    def columns(kind):
        return lambda i, blk, ids: (0, 0, blk[kind * line + jnp.minimum(i, line - 1)])

    own, sent, stats = run_kernel(
        functools.partial(regroup_body, micro=micro, tok=tok),
        [
            (
                (2, tokens, line * rows),
                BF16,
                (2, tokens, rows),
                lambda i, *_: (0, 0, jnp.minimum(i, line - 1)),
            ),
            ((2, tokens, (line + 1) * rows), BF16, (2, tokens, rows), lambda i, *_: (0, 0, i)),
            ((tokens, 256), F32),
        ],
        [
            (value, (micro, tok, rows), columns(kind))
            for value in (history[0], codes[0], cotangent)
            for kind in (0, 1)
        ]
        + [scales[0][..., None]],
        grid=(line + 1,),
        scalars=(blocks, sample_ids[0]),
        scratch=[pltpu.VMEM((2 * line, tokens, rows), BF16)],
    )
    sib = sibling(after(sent, *nears[0], ups[1]))
    stats_sib = (sib, (1, tokens, 128), lambda i, *_: (0, 0, line * rows // 128))

    ups.append(along(ups[1]))
    downs.append(along(after(downs[0], ups[1])))
    nears.append(both(ups[1]))
    def part(value, index):
        return (value, (2, tokens, rows), lambda i, *_: (0, 0, index))

    def one(value, kind, index):
        return (value, (1, tokens, rows), lambda i, *_: (kind, 0, index))

    def feature(value, index):
        return (value, (1, rows), lambda i, blk: (0, blk[index]))

    def add_step(sums, index, gathered):
        first = index == 0
        args = [
            part(own, index),
            part(sib, index),
            stats,
            stats_sib,
            feature(gain, index),
            feature(bias, index),
            downs[index],
            ups[index],
            *gathered,
        ]
        shapes = [
            ((tokens, (1 + sections) * rank), F32),
            ((tokens, (1 + sections) * rank), F32),
            ((rank + 8, (sections - 1) * rank), F32),
        ]
        return run_kernel(
            functools.partial(step_body, first=first, sections=sections),
            shapes,
            args + list(sums),
            scalars=(blocks,),
            aliases=None if first else {13 + i: i for i in range(3)},
            limit=28 * 1024 * 1024,
        )

    firsts = [first_half(nears[0][0], *nears[1])]
    ups.append(along(ups[2]))
    downs.append(along(downs[1]))
    nears.append(both(after(ups[2], *nears[1], sib)))
    seconds = [second_half(nears[0][1], *nears[2])]
    firsts.append(first_half(nears[1][0], *nears[2]))
    seconds.append(second_half(nears[1][1], *nears[2]))
    sums = add_step((), 0, nears[0] + (firsts[0], seconds[0]))
    nears.append(both(after(ups[3], *nears[2], *firsts, *seconds, *sums)))
    for index in range(2, line):
        firsts.append(first_half(nears[index][0]))
        seconds.append(second_half(nears[index][1]))
    (normed,) = run_kernel(
        norm_body,
        [((2 * tokens, rows), BF16)],
        [
            one(own, 0, 1),
            one(sib, 0, 1),
            stats,
            stats_sib,
            feature(gain, 1),
            feature(bias, 1),
        ],
        scalars=(blocks,),
    )
    downs.append(along(downs[2]))
    for index in range(1, line):
        sums = add_step(after(sums, normed), index, nears[index] + (firsts[index], seconds[index]))
    mine, other, cross = sums
    normed_ahead = along(after(normed, mine), -1)

    got, cross_got = sibling(other), sibling(cross)

    apart = sections - 1
    small, shared, spread, projected, kappa, to_next, to_rest = run_kernel(
        functools.partial(open_body, width=width),
        [
            ((tokens, 2 * rank), F32),
            ((tokens, 2 * rank), F32),
            ((tokens, apart * rank), F32),
            ((rank, apart * rank), BF16),
            ((8, rank), F32),
            ((tokens, rank), BF16),
            ((tokens, 2 * rank), BF16),
        ],
        [mine, got, cross, cross_got, stats],
    )
    arrivals = [lax.ppermute(to_next, "section", [(3, 2)])]
    late = lax.ppermute(to_rest, "section", [(3, 1)])
    state = [small, shared, spread, projected, kappa, stats]
    for turn in (1, 2, 3):
        (passed,) = run_kernel(
            functools.partial(chain_body, width=width, turn=turn),
            [((tokens, 2 * rank if turn == 1 else rank), BF16)],
            state + arrivals,
        )
        if turn == 1:
            arrivals += [late, lax.ppermute(passed, "section", [(2, 1)])]
        elif turn == 2:
            arrivals += [lax.ppermute(passed, "section", [(1, 0)])]
    act = passed
    act_sib, shared_sib = sibling(act), sibling(shared)

    scale = 1.0 / tok
    level = section.astype(jnp.int32).reshape(1)

    def grad_block(index, act):
        outs = [((2 * tokens, rows), BF16)]
        if index != 1:
            outs.append(((rows, rank), BF16))
        return run_kernel(
            functools.partial(grad_body, scale=scale, width=width, index=index),
            outs,
            [
                (own, None),
                (sib, None),
                stats,
                stats_sib,
                act,
                act_sib,
                shared,
                shared_sib,
                kappa,
                feature(gain, index),
                feature(bias, index),
                downs[index],
            ],
            scalars=(blocks,),
            scratch=[pltpu.VMEM((2, tokens, rows), BF16), pltpu.SemaphoreType.DMA((2,))],
        )

    def close_block(index, arrived):
        return run_kernel(
            functools.partial(close_body, scale=scale, count=len(arrived), index=index),
            [((tokens, rows), BF16), ((tokens, rows), BF16), ((rows, rank), BF16)],
            [(own, None), (sib, None), shared, shared_sib, terms[index], *arrived],
            scalars=(level,),
            scratch=[pltpu.VMEM((2, tokens, rows), BF16), pltpu.SemaphoreType.DMA((2,))],
        )

    terms, down_grads, up_grads, mines, theirs = {}, {}, {}, {}, {}
    act_sib = after(act_sib, normed_ahead)
    (terms[1],) = grad_block(1, act)
    act = after(act, terms[1])
    terms[2], *down_grads[2] = grad_block(2, act)
    terms[3], *down_grads[3] = grad_block(3, act)
    act_ahead = along(jnp.concatenate(after([act, act_sib], terms[3]), axis=0), -1)

    def add(*values):
        return sum(value.astype(F32) for value in values)

    def pass_on(running, part):
        return along(add(running, part).astype(BF16))

    def scan_open(index):
        return lax.ppermute(terms[index], "section", [(3, 2), (1, 0), (2, 3)])

    def scan_pairs(*pairs):
        return lax.ppermute(terms[1], "section", pairs)

    def scan_sum(index, arrived):
        return add(terms[index], arrived).astype(BF16)

    def scan_more(value):
        return lax.ppermute(value, "section", [(3, 1), (2, 0)])

    opened = {1: scan_pairs((3, 2), (2, 3))}
    beside = scan_pairs((1, 0))
    opened.update({index: scan_open(index) for index in (2, 3)})
    down_ring = along(down_grads[2][0])
    sums = {1: scan_sum(1, after(opened[1], terms[2], terms[3]))}
    more = {1: scan_more(sums[1])}
    down_sum = add(after(down_ring, beside, act_ahead), down_grads[3][0]).astype(BF16)
    down_ring = along(down_sum)
    sums[2] = scan_sum(2, after(opened[2], more[1]))
    more[2] = scan_more(sums[2])
    mines[1], theirs[1], up_grads[1] = close_block(
        1, (opened[1], after(more[1], down_sum, sums[2]), beside)
    )
    up_ring = along(up_grads[1])
    terms[0], *down_grads[0] = grad_block(0, after(act, up_grads[1]))
    opened[0] = scan_open(0)
    sums[3] = scan_sum(3, after(opened[3], sums[2], up_grads[1]))
    more[3] = scan_more(sums[3])
    mines[2], theirs[2], up_grads[2] = close_block(
        2, (opened[2], after(more[2], sums[3], down_ring))
    )
    more[0] = scan_more(scan_sum(0, after(opened[0], sums[3], up_grads[2])))
    halves = [slice(0, rows // 2), slice(rows // 2, rows)]
    up_sums = [add(up_ring[half], up_grads[2][half]).astype(BF16) for half in halves]
    up_ring = [along(value) for value in up_sums]
    mines[3], theirs[3], up_grads[3] = close_block(3, (opened[3], after(more[3], *up_sums)))
    up_sums = [add(up_ring[0], up_grads[3][halves[0]]).astype(BF16)]
    second = after(up_ring[1], up_sums[0])
    up_sums.append(add(second, up_grads[3][halves[1]]).astype(BF16))
    up_ring = [along(value) for value in up_sums]

    def place(first, count, produced):
        sent = [theirs[index] for index in range(first, first + count)]
        arrived = sibling(jnp.concatenate(sent, axis=1) if count > 1 else sent[0])
        args = [mines[index] for index in range(first, first + count)]
        args.append((arrived, (tokens, rows), lambda i, blk: (0, jnp.maximum(i - count, 0))))
        if produced is not None:
            args.append((produced, None))

        def target(i, blk):
            return (0, blk[first + jnp.where(i < count, i, line + i - count)])

        return run_kernel(
            functools.partial(place_body, count=count),
            [((tokens, width), BF16, (tokens, rows), target)],
            args,
            grid=(2 * count,),
            scalars=(blocks,),
            aliases=None if produced is None else {len(args): 0},
        )[0]

    produced = place(1, line - 1, None)
    mines[0], theirs[0], up_grads[0] = close_block(
        0, (opened[0], after(more[0], up_ring[0], up_sums[1], produced))
    )
    produced = place(0, 1, produced)
    (down_own,) = run_kernel(
        functools.partial(ahead_body, scale=scale),
        [((rows, rank), F32)],
        [normed_ahead, act_ahead, after(down_grads[0][0], mines[3])],
    )
    up_sum = add(jnp.concatenate(up_ring, axis=0), up_grads[0])
    grads = jnp.concatenate([add(down_ring, down_own), up_sum], axis=1)
    return produced.reshape(1, micro, tok, width), grads[None]


def solution(mesh):
    def run(*args):
        rows = args[7].shape[1] // mesh.shape["rep"]
        split = mesh.shape["section"] == 4 and mesh.shape["rep"] == 8 and rows % 128 == 0
        body = per_device if split else plain_device
        return jax.shard_map(
            body,
            mesh=mesh,
            in_specs=(
                P("section", "rep", None, None),
                P("section", "rep", None, None),
                P("section", "rep", None),
                P("rep", None),
                P("rep", None, None),
                P("section", None),
                P("section", None),
                P("section", "rep", None),
                P("section", "rep", None),
            ),
            out_specs=(P("section", "rep", None, None), P("section", "rep", None)),
            check_vma=False,
        )(*args)

    return run
```

```python
import functools

import jax
import jax.numpy as jnp
from jax import lax
from jax.experimental import pallas as pl
from jax.experimental.pallas import tpu as pltpu
from jax.sharding import PartitionSpec as P

EPSILON = 1e-05
HALF_ROOT = 0.7071067811865476
DENSITY = 0.3989422804014327


def from_behind(value, axis, steps):
    count = lax.axis_size(axis)
    leading, last = (max(0, -steps), min(count, count - steps))
    return lax.ppermute(value, axis, [(source, source + steps) for source in range(leading, last)])


def unpack_codes(levels):
    return levels.astype(jnp.float32)


def gelu_pair(preact):
    normal_cdf = 0.5 * (1.0 + lax.erf(preact * HALF_ROOT))
    bump = DENSITY * jnp.exp(-0.5 * preact * preact)
    return (preact * normal_cdf, normal_cdf + preact * bump)


def section_inputs(stored, packed, scaling, picks):
    chosen = jnp.take(stored, picks, axis=0).astype(jnp.float32)
    rebuilt = chosen + scaling[..., None] * unpack_codes(packed)
    return rebuilt.astype(jnp.bfloat16).reshape(-1, stored.shape[-1])


def normalize(inputs, gain_row, bias_row):
    values = inputs.astype(jnp.float32)
    centred = values - jnp.mean(values, axis=-1, keepdims=True)
    inv_std = lax.rsqrt(jnp.mean(centred * centred, axis=-1, keepdims=True) + EPSILON)
    scaled = centred * inv_std
    normed = (scaled * gain_row + bias_row).astype(jnp.bfloat16)
    return (normed, scaled, inv_std)


def input_grad(out_grad, back, gain_row, scaled, inv_std):
    weighted = back * gain_row
    inner = (
        weighted
        - jnp.mean(weighted, axis=-1, keepdims=True)
        - scaled * jnp.mean(weighted * scaled, axis=-1, keepdims=True)
    )
    return (out_grad.astype(jnp.float32) + inv_std * inner).astype(jnp.bfloat16)


def contract_rows(left, right):
    return lax.dot_general(
        left, right, (((0,), (0,)), ((), ())), preferred_element_type=jnp.float32
    )


def contract_cols(left, right):
    return lax.dot_general(
        left, right, (((1,), (1,)), ((), ())), preferred_element_type=jnp.float32
    )


def take_rows(source, begin, count):
    return lax.dynamic_slice_in_dim(source, begin, count, 0)


def put_rows(target, active, values, begin):
    older = lax.dynamic_slice_in_dim(target, begin, values.shape[0], 0)
    return lax.dynamic_update_slice_in_dim(target, jnp.where(active, values, older), begin, 0)


def plain_device(
    history, codes, scales, sample_ids, cotangent, ln_gain, ln_bias, down_weight, up_weight
):
    sections = lax.axis_size("section")
    position = lax.axis_index("section")
    w_down, w_up = (
        lax.all_gather(down_weight[0], "rep", axis=0, tiled=True),
        lax.all_gather(up_weight[0], "rep", axis=0, tiled=True),
    )
    inputs = section_inputs(history[0], codes[0], scales[0], sample_ids[0])
    gain_row = ln_gain[0]
    bias_row = ln_bias[0]
    normed, scaled, inv_std = normalize(inputs, gain_row, bias_row)
    activated, slopes = gelu_pair(jnp.dot(normed, w_down, preferred_element_type=jnp.float32))
    hidden = activated.astype(jnp.bfloat16)
    tok_count = cotangent.shape[1]
    row_total = inputs.shape[0]
    model_width = inputs.shape[1]
    rank_pair = 2 * w_down.shape[1]
    seeded = cotangent.reshape(row_total, model_width)
    pieces = 1
    block_size = tok_count // pieces
    blocks = row_total // block_size
    tick_count = blocks + sections - 1

    def advance(tick, carry):
        incoming, produced, running, kept_grad, kept_top = carry
        offset = tick - (sections - 1 - position)
        active = jnp.logical_and(offset >= 0, offset < blocks)
        begin = jnp.clip(offset, 0, blocks - 1) * block_size
        top_grad = take_rows(seeded, begin, block_size)
        out_grad = jnp.where(position == sections - 1, top_grad, incoming)
        slope_rows = take_rows(slopes, begin, block_size)
        scaled_rows = take_rows(scaled, begin, block_size)
        inv_rows = take_rows(inv_std, begin, block_size)
        act_grad = (
            jnp.dot(out_grad, w_up, preferred_element_type=jnp.float32) * slope_rows
        ).astype(jnp.bfloat16)
        back = contract_cols(act_grad, w_down)
        result = input_grad(out_grad, back, gain_row, scaled_rows, inv_rows)
        produced = put_rows(produced, active, result, begin)
        normed_rows = take_rows(normed, begin, block_size)
        hidden_rows = take_rows(hidden, begin, block_size)
        terms = jnp.concatenate(
            [contract_rows(normed_rows, act_grad), contract_rows(out_grad, hidden_rows)], axis=1
        )
        running = running + jnp.where(active, terms, 0.0)
        incoming = from_behind(result, "section", -1)
        return (incoming, produced, running, kept_grad, kept_top)

    start_in = jnp.zeros((block_size, model_width), jnp.bfloat16)
    start_out = jnp.zeros((row_total, model_width), jnp.bfloat16)
    start_sum = jnp.zeros((model_width, rank_pair), jnp.float32)
    start_grad = jnp.zeros((1, 1), jnp.bfloat16)
    start_top = jnp.zeros((1, 1), jnp.bfloat16)
    carry = lax.fori_loop(
        0, tick_count, advance, (start_in, start_out, start_sum, start_grad, start_top)
    )
    produced = carry[1]
    summed = lax.psum_scatter(
        (carry[2] / float(tok_count)).astype(jnp.bfloat16), "rep", scatter_dimension=0, tiled=True
    ).astype(jnp.float32)
    return (produced.reshape(1, row_total // tok_count, tok_count, model_width), summed[None])


VMEM_LIMIT = 16 * 1024 * 1024
F32 = jnp.float32
BF16 = jnp.bfloat16


def run_kernel(body, outs, args, grid=(1,), scalars=(), scratch=(), aliases=None, limit=VMEM_LIMIT):
    def whole(shape):
        return pl.BlockSpec(shape, lambda *_: (0,) * len(shape))

    arrays, in_specs, out_specs, out_shapes = [], [], [], []
    for arg in args:
        if isinstance(arg, tuple) and arg[1] is None:
            arrays.append(arg[0])
            in_specs.append(pl.BlockSpec(memory_space=pltpu.HBM))
        elif isinstance(arg, tuple):
            arrays.append(arg[0])
            in_specs.append(pl.BlockSpec(arg[1], arg[2]))
        else:
            arrays.append(arg)
            in_specs.append(whole(arg.shape))
    for out in outs:
        out_shapes.append(jax.ShapeDtypeStruct(out[0], out[1]))
        out_specs.append(pl.BlockSpec(out[2], out[3]) if len(out) > 2 else whole(out[0]))
    return pl.pallas_call(
        body,
        out_shape=out_shapes,
        grid_spec=pltpu.PrefetchScalarGridSpec(
            num_scalar_prefetch=len(scalars),
            grid=grid,
            in_specs=in_specs,
            out_specs=out_specs,
            scratch_shapes=list(scratch),
        ),
        input_output_aliases=aliases or {},
        compiler_params=pltpu.CompilerParams(vmem_limit_bytes=limit),
        cost_estimate=pl.CostEstimate(flops=0, bytes_accessed=0, transcendentals=0),
    )(*scalars, *arrays)


def regroup_body(
    blocks, picks, hist0, hist1, code0, code1, cot0, cot1, step, own, sent, stats, kept, *, micro, tok
):
    place = pl.program_id(0)
    last = pl.num_programs(0) - 1

    @pl.when(place < last)
    def _():
        for which, (hist, code, cot, out) in enumerate(
            ((hist0, code0, cot0, own), (hist1, code1, cot1, sent))
        ):
            for m in range(micro):
                rows = pl.ds(m * tok, tok)
                rebuilt = hist[picks[m]].astype(F32) + step[m] * code[m].astype(F32)
                rebuilt = rebuilt.astype(BF16)
                out[0, rows, :] = rebuilt
                out[1, rows, :] = cot[m]
                kept[2 * place + which, rows, :] = rebuilt

    @pl.when(place == last)
    def _():
        total, rows, lanes = kept.shape
        width = total * lanes

        def add(index, acc):
            return acc + jnp.sum(kept[index].astype(F32), axis=-1, keepdims=True)

        mean = lax.fori_loop(0, total, add, jnp.zeros((rows, 1), F32)) / width

        def add_square(index, acc):
            centred = kept[index].astype(F32) - mean
            return acc + jnp.sum(centred * centred, axis=-1, keepdims=True)

        var = lax.fori_loop(0, total, add_square, jnp.zeros((rows, 1), F32)) / width
        inv_std = lax.rsqrt(var + EPSILON)
        half = stats.shape[1] // 2
        stats[:, :half] = jnp.broadcast_to(mean, (rows, half))
        stats[:, half:] = jnp.broadcast_to(inv_std, (rows, half))
        lane = lax.broadcasted_iota(jnp.int32, (rows, 128), 1)
        packed = jnp.zeros((rows, 128), F32)
        for index, value in enumerate(bf16_parts(mean) + bf16_parts(inv_std)):
            packed = jnp.where(lane == index, value, packed)
        sent[0, :, :128] = packed.astype(BF16)


def bf16_parts(value):
    parts = []
    for _ in range(3):
        parts.append(value.astype(BF16).astype(F32))
        value = value - parts[-1]
    return parts


def split_stats(stats):
    if len(stats.shape) == 3:
        parts = stats[0].astype(F32)
        return [sum(parts[:, i : i + 1] for i in range(k, k + 3)) for k in (0, 3)]
    half = stats.shape[1] // 2
    return stats[:, 0:1], stats[:, half : half + 1]


def norm_body(blocks, own, sib, stats_own, stats_sib, gain, bias, out):
    tokens = own.shape[1]
    for slot, (values, stats) in enumerate(((own, stats_own), (sib, stats_sib))):
        mean, inv_std = split_stats(stats)
        scaled = (values[0].astype(F32) - mean) * inv_std
        out[slot * tokens : (slot + 1) * tokens, :] = (scaled * gain[...] + bias[...]).astype(BF16)


def as_column(row, lanes):
    turned = jnp.transpose(jnp.broadcast_to(row, (128, row.shape[1])))
    return jnp.concatenate([turned] * (lanes // 128), axis=1)


def step_body(*refs, first, sections):
    refs = refs[1:]
    own, sib, stats_own, stats_sib, gain, bias, down, up, near, far, diag_a, diag_b = refs[:12]
    refs = refs[12:]
    if first:
        old = None
        outs = refs
    else:
        old, outs = refs[:3], refs[3:]
    rank = down.shape[1]
    tokens = own.shape[1]
    weights = down[...]
    gain_row, bias_row = gain[...], bias[...]
    others = [near[...], far[...], jnp.concatenate([diag_a[...], diag_b[...]], axis=0)]
    for slot, (values, stats) in enumerate(((own, stats_own), (sib, stats_sib))):
        mean, inv_std = split_stats(stats)
        inputs = values[0]
        scaled = (inputs.astype(F32) - mean) * inv_std
        normed = (scaled * gain_row + bias_row).astype(BF16)
        pieces = [
            jnp.dot(values[1], up[...], preferred_element_type=F32),
            jnp.dot(normed, weights, preferred_element_type=F32),
        ] + [jnp.dot(inputs, other, preferred_element_type=F32) for other in others]
        for index, piece in enumerate(pieces):
            columns = slice(index * rank, (index + 1) * rank)
            if old is not None:
                piece = piece + old[slot][:, columns]
            outs[slot][:, columns] = piece
    wide = weights.astype(F32)
    gained = wide * as_column(gain_row, rank)
    biased = wide * as_column(bias_row, rank)
    gained_low = gained.astype(BF16)
    cross = outs[2]

    def put(rows, columns, value):
        if old is not None:
            value = value + old[2][rows, columns]
        cross[rows, columns] = value

    for index, other in enumerate(others):
        columns = slice(index * rank, (index + 1) * rank)
        put(slice(0, rank), columns, contract_rows(gained_low, other))
        put(
            slice(rank, rank + 1),
            columns,
            jnp.sum(other.astype(F32), axis=0, keepdims=True),
        )
    put(slice(rank + 1, rank + 2), slice(0, rank), jnp.sum(gained, axis=0, keepdims=True))
    put(slice(rank + 1, rank + 2), slice(rank, 2 * rank), jnp.sum(biased, axis=0, keepdims=True))


def chain_values(pre, slopes, centred, spread, cross, kappa, inv_std, width):
    act_grad = (pre * slopes).astype(BF16)
    wide = act_grad.astype(F32)
    second = jnp.sum(wide * centred, axis=-1, keepdims=True) / width
    return inv_std * (jnp.dot(act_grad, cross, preferred_element_type=F32) - second * spread)


def open_body(
    mine, got, cross, cross_got, stats, small, shared, spread_out, cross_out, kappa_out, near, rest, *, width
):
    rank = near.shape[1]
    total = mine[...] + got[...]
    both = cross[...] + cross_got[...]
    mean, inv_std = split_stats(stats)
    base = total[:, :rank]
    preact = total[:, rank : 2 * rank]
    sums = both[rank : rank + 1, :]
    kappa = both[rank + 1 : rank + 2, :rank]
    beta = both[rank + 1 : rank + 2, rank : 2 * rank]
    activated, slopes = gelu_pair(preact)
    centred = preact - beta
    spread = inv_std * (total[:, 2 * rank :] - mean * sums)
    kappa_column = as_column(kappa, rank)[:, 0:1]
    projected = (both[:rank, :] - kappa_column * (sums / width)).astype(BF16)
    small[:, :rank] = base
    small[:, rank:] = slopes
    shared[:, :rank] = activated
    shared[:, rank:] = centred
    spread_out[...] = spread
    cross_out[...] = projected
    kappa_out[...] = jnp.broadcast_to(kappa, kappa_out.shape)
    values = chain_values(base, slopes, centred, spread, projected, kappa, inv_std, width)
    near[...] = values[:, :rank].astype(BF16)
    rest[...] = values[:, rank:].astype(BF16)


def chain_body(*refs, width, turn):
    small, shared, spread, cross, kappa, stats = refs[:6]
    arrivals, out = refs[6:-1], refs[-1]
    rank = cross.shape[0]
    _, inv_std = split_stats(stats)
    pre = small[:, :rank]
    for arrival in arrivals:
        pre = pre + arrival[:, :rank].astype(F32)
    slopes = small[:, rank:]
    if turn == 3:
        out[...] = (pre * slopes).astype(BF16)
        return
    values = chain_values(
        pre, slopes, shared[:, rank:], spread[...], cross[...], kappa[0:1, :], inv_std, width
    )
    if turn == 1:
        out[:, :rank] = values[:, 2 * rank :].astype(BF16)
        out[:, rank:] = values[:, rank : 2 * rank].astype(BF16)
        return
    passed = arrivals[1][:, rank:].astype(F32) + arrivals[2][:, rank:].astype(F32)
    out[...] = (values[:, :rank] + passed).astype(BF16)


def grad_body(*refs, scale, width, index):
    *refs, held, sems = refs
    columns = pl.ds(index * held.shape[2], held.shape[2])
    copies = [
        pltpu.make_async_copy(source.at[0, :, columns], held.at[slot], sems.at[slot])
        for slot, source in enumerate(refs[1:3])
    ]
    for copy in copies:
        copy.start()
    stats_own, stats_sib, act_own, act_sib, shared_own, shared_sib, kappa = refs[3:10]
    gain, bias, down, term, *grads = refs[10:]
    gain_row, bias_row = gain[...], bias[...]
    weights = down[...]
    rank = weights.shape[1]
    total = None
    for slot, (stats, act, shared) in enumerate(
        ((stats_own, act_own, shared_own), (stats_sib, act_sib, shared_sib))
    ):
        mean, inv_std = split_stats(stats)
        act_grad = act[...]
        wide = act_grad.astype(F32)
        first = jnp.sum(wide * kappa[0:1, :], axis=-1, keepdims=True) / width
        second = jnp.sum(wide * shared[:, rank:], axis=-1, keepdims=True) / width
        copies[slot].wait()
        scaled = (held[slot].astype(F32) - mean) * inv_std
        normed = (scaled * gain_row + bias_row).astype(BF16)
        weighted = contract_cols(act_grad, weights) * gain_row
        tokens = act_grad.shape[0]
        term[slot * tokens : (slot + 1) * tokens, :] = (
            inv_std * (weighted - first - scaled * second)
        ).astype(BF16)
        piece = contract_rows(normed, act_grad)
        total = piece if total is None else total + piece
    for grad in grads:
        grad[...] = (total * scale).astype(BF16)


def ahead_body(normed, act, own, out, *, scale):
    out[...] = own[...].astype(F32) + contract_rows(normed[...], act[...]) * scale


def close_body(*refs, scale, count, index):
    *refs, held, sems = refs
    columns = pl.ds(index * held.shape[2], held.shape[2])
    copies = [
        pltpu.make_async_copy(source.at[1, :, columns], held.at[slot], sems.at[slot])
        for slot, source in enumerate(refs[1:3])
    ]
    for copy in copies:
        copy.start()
    level, _, _, shared_own, shared_sib, term = refs[0:6]
    arrivals = refs[6 : 6 + count]
    mine, theirs, grad = refs[6 + count :]
    rank = grad.shape[1]
    total = None
    for slot, (shared, out) in enumerate(((shared_own, mine), (shared_sib, theirs))):
        tokens = shared.shape[0]
        rows = slice(slot * tokens, (slot + 1) * tokens)
        copies[slot].wait()
        arrived = held[slot].astype(F32)
        for place, arrival in enumerate(arrivals):
            values = arrival[rows, :].astype(F32)
            if place == 0:
                values = jnp.where(level[0] % 2 == 0, values, 0.0)
            arrived = arrived + values
        out_grad = arrived.astype(BF16)
        out[...] = (out_grad.astype(F32) + term[rows, :].astype(F32)).astype(BF16)
        piece = contract_rows(out_grad, shared[:, :rank].astype(BF16))
        total = piece if total is None else total + piece
    grad[...] = (total * scale).astype(BF16)


def place_body(blocks, *refs, count):
    mines, arrived, out = refs[:count], refs[count], refs[-1]
    place = pl.program_id(0)
    for index, source in enumerate(mines):

        @pl.when(place == index)
        def _():
            out[...] = source[...]

    @pl.when(place >= count)
    def _():
        out[...] = arrived[...]


def per_device(
    history, codes, scales, sample_ids, cotangent, ln_gain, ln_bias, down_weight, up_weight
):
    sections = lax.axis_size("section")
    reps = lax.axis_size("rep")
    line = reps // 2
    section = lax.axis_index("section")
    rep = lax.axis_index("rep")
    chip, core = rep // 2, rep % 2
    _, micro, tok, width = history.shape
    tokens = micro * tok
    rows, rank = down_weight.shape[1:]

    def sibling(value):
        return lax.ppermute(value, "rep", [(r, r ^ 1) for r in range(reps)])

    def along(value, steps=1):
        return lax.ppermute(value, "rep", [(r, (r + 2 * steps) % reps) for r in range(reps)])

    def flip(value, mask):
        return lax.ppermute(value, "section", [(s, s ^ mask) for s in range(sections)])

    def after(value, *first):
        return lax.optimization_barrier((value, first))[0]

    chips = (chip - jnp.arange(line, dtype=jnp.int32)) % line
    blocks = jnp.concatenate([2 * chips + core, 2 * chips + 1 - core]).astype(jnp.int32)
    gain, bias = ln_gain, ln_bias

    ups, downs = [up_weight[0]], [down_weight[0]]
    cut = rows // 2

    def both(value):
        return flip(value, 1), flip(value, 2)

    def first_half(near, *first):
        return flip(after(near, *first)[:cut], 2)

    def second_half(far, *first):
        return flip(after(far, *first)[cut:], 1)

    nears = [both(ups[0])]
    ups.append(along(ups[0]))

    def columns(kind):
        return lambda i, blk, ids: (0, 0, blk[kind * line + jnp.minimum(i, line - 1)])

    own, sent, stats = run_kernel(
        functools.partial(regroup_body, micro=micro, tok=tok),
        [
            (
                (2, tokens, line * rows),
                BF16,
                (2, tokens, rows),
                lambda i, *_: (0, 0, jnp.minimum(i, line - 1)),
            ),
            ((2, tokens, (line + 1) * rows), BF16, (2, tokens, rows), lambda i, *_: (0, 0, i)),
            ((tokens, 256), F32),
        ],
        [
            (value, (micro, tok, rows), columns(kind))
            for value in (history[0], codes[0], cotangent)
            for kind in (0, 1)
        ]
        + [scales[0][..., None]],
        grid=(line + 1,),
        scalars=(blocks, sample_ids[0]),
        scratch=[pltpu.VMEM((2 * line, tokens, rows), BF16)],
    )
    sib = sibling(after(sent, *nears[0], ups[1]))
    stats_sib = (sib, (1, tokens, 128), lambda i, *_: (0, 0, line * rows // 128))

    ups.append(along(ups[1]))
    downs.append(along(after(downs[0], ups[1])))
    nears.append(both(ups[1]))
    def part(value, index):
        return (value, (2, tokens, rows), lambda i, *_: (0, 0, index))

    def one(value, kind, index):
        return (value, (1, tokens, rows), lambda i, *_: (kind, 0, index))

    def feature(value, index):
        return (value, (1, rows), lambda i, blk: (0, blk[index]))

    def add_step(sums, index, gathered):
        first = index == 0
        args = [
            part(own, index),
            part(sib, index),
            stats,
            stats_sib,
            feature(gain, index),
            feature(bias, index),
            downs[index],
            ups[index],
            *gathered,
        ]
        shapes = [
            ((tokens, (1 + sections) * rank), F32),
            ((tokens, (1 + sections) * rank), F32),
            ((rank + 8, (sections - 1) * rank), F32),
        ]
        return run_kernel(
            functools.partial(step_body, first=first, sections=sections),
            shapes,
            args + list(sums),
            scalars=(blocks,),
            aliases=None if first else {13 + i: i for i in range(3)},
            limit=28 * 1024 * 1024,
        )

    firsts = [first_half(nears[0][0], *nears[1])]
    ups.append(along(ups[2]))
    downs.append(along(downs[1]))
    nears.append(both(after(ups[2], *nears[1], sib)))
    seconds = [second_half(nears[0][1], *nears[2])]
    firsts.append(first_half(nears[1][0], *nears[2]))
    seconds.append(second_half(nears[1][1], *nears[2]))
    sums = add_step((), 0, nears[0] + (firsts[0], seconds[0]))
    nears.append(both(after(ups[3], *nears[2], *firsts, *seconds, *sums)))
    for index in range(2, line):
        firsts.append(first_half(nears[index][0]))
        seconds.append(second_half(nears[index][1]))
    (normed,) = run_kernel(
        norm_body,
        [((2 * tokens, rows), BF16)],
        [
            one(own, 0, 1),
            one(sib, 0, 1),
            stats,
            stats_sib,
            feature(gain, 1),
            feature(bias, 1),
        ],
        scalars=(blocks,),
    )
    downs.append(along(downs[2]))
    for index in range(1, line):
        sums = add_step(after(sums, normed), index, nears[index] + (firsts[index], seconds[index]))
    mine, other, cross = sums
    normed_ahead = along(after(normed, mine), -1)

    got, cross_got = sibling(other), sibling(cross)

    apart = sections - 1
    small, shared, spread, projected, kappa, to_next, to_rest = run_kernel(
        functools.partial(open_body, width=width),
        [
            ((tokens, 2 * rank), F32),
            ((tokens, 2 * rank), F32),
            ((tokens, apart * rank), F32),
            ((rank, apart * rank), BF16),
            ((8, rank), F32),
            ((tokens, rank), BF16),
            ((tokens, 2 * rank), BF16),
        ],
        [mine, got, cross, cross_got, stats],
    )
    arrivals = [lax.ppermute(to_next, "section", [(3, 2)])]
    late = lax.ppermute(to_rest, "section", [(3, 1)])
    state = [small, shared, spread, projected, kappa, stats]
    for turn in (1, 2, 3):
        (passed,) = run_kernel(
            functools.partial(chain_body, width=width, turn=turn),
            [((tokens, 2 * rank if turn == 1 else rank), BF16)],
            state + arrivals,
        )
        if turn == 1:
            arrivals += [late, lax.ppermute(passed, "section", [(2, 1)])]
        elif turn == 2:
            arrivals += [lax.ppermute(passed, "section", [(1, 0)])]
    act = passed
    act_sib, shared_sib = sibling(act), sibling(shared)

    scale = 1.0 / tok
    level = section.astype(jnp.int32).reshape(1)

    def grad_block(index, act):
        outs = [((2 * tokens, rows), BF16)]
        if index != 1:
            outs.append(((rows, rank), BF16))
        return run_kernel(
            functools.partial(grad_body, scale=scale, width=width, index=index),
            outs,
            [
                (own, None),
                (sib, None),
                stats,
                stats_sib,
                act,
                act_sib,
                shared,
                shared_sib,
                kappa,
                feature(gain, index),
                feature(bias, index),
                downs[index],
            ],
            scalars=(blocks,),
            scratch=[pltpu.VMEM((2, tokens, rows), BF16), pltpu.SemaphoreType.DMA((2,))],
        )

    def close_block(index, arrived):
        return run_kernel(
            functools.partial(close_body, scale=scale, count=len(arrived), index=index),
            [((tokens, rows), BF16), ((tokens, rows), BF16), ((rows, rank), BF16)],
            [(own, None), (sib, None), shared, shared_sib, terms[index], *arrived],
            scalars=(level,),
            scratch=[pltpu.VMEM((2, tokens, rows), BF16), pltpu.SemaphoreType.DMA((2,))],
        )

    terms, down_grads, up_grads, mines, theirs = {}, {}, {}, {}, {}
    act_sib = after(act_sib, normed_ahead)
    (terms[1],) = grad_block(1, act)
    act = after(act, terms[1])
    terms[2], *down_grads[2] = grad_block(2, act)
    terms[3], *down_grads[3] = grad_block(3, act)

    def add(*values):
        return sum(value.astype(F32) for value in values)

    def pass_on(running, part):
        return along(add(running, part).astype(BF16))

    def scan_open(index):
        return lax.ppermute(terms[index], "section", [(3, 2), (1, 0), (2, 3)])

    def scan_pairs(*pairs):
        return lax.ppermute(terms[1], "section", pairs)

    def scan_sum(index, arrived):
        return add(terms[index], arrived).astype(BF16)

    def scan_more(value):
        return lax.ppermute(value, "section", [(3, 1), (2, 0)])

    opened = {1: scan_pairs((3, 2), (2, 3))}
    beside = scan_pairs((1, 0))
    opened.update({index: scan_open(index) for index in (2, 3)})
    down_ring = along(down_grads[2][0])
    sums = {1: scan_sum(1, after(opened[1], terms[2], terms[3]))}
    more = {1: scan_more(sums[1])}
    act_ahead = along(jnp.concatenate(after([act, act_sib], sums[1]), axis=0), -1)
    down_sum = add(after(down_ring, beside), down_grads[3][0]).astype(BF16)
    down_ring = along(down_sum)
    sums[2] = scan_sum(2, after(opened[2], more[1], act_ahead))
    more[2] = scan_more(sums[2])
    mines[1], theirs[1], up_grads[1] = close_block(
        1, (opened[1], after(more[1], down_sum, sums[2]), beside)
    )
    up_ring = along(up_grads[1])
    terms[0], *down_grads[0] = grad_block(0, after(act, up_grads[1]))
    opened[0] = scan_open(0)
    sums[3] = scan_sum(3, after(opened[3], sums[2], up_grads[1]))
    more[3] = scan_more(sums[3])
    mines[2], theirs[2], up_grads[2] = close_block(
        2, (opened[2], after(more[2], sums[3], down_ring))
    )
    more[0] = scan_more(scan_sum(0, after(opened[0], sums[3], up_grads[2])))
    halves = [slice(0, rows // 2), slice(rows // 2, rows)]
    up_sums = [add(up_ring[half], up_grads[2][half]).astype(BF16) for half in halves]
    up_ring = [along(value) for value in up_sums]
    mines[3], theirs[3], up_grads[3] = close_block(3, (opened[3], after(more[3], *up_sums)))
    up_sums = [add(up_ring[0], up_grads[3][halves[0]]).astype(BF16)]
    second = after(up_ring[1], up_sums[0])
    up_sums.append(add(second, up_grads[3][halves[1]]).astype(BF16))
    up_ring = [along(value) for value in up_sums]

    def place(first, count, produced):
        sent = [theirs[index] for index in range(first, first + count)]
        arrived = sibling(jnp.concatenate(sent, axis=1) if count > 1 else sent[0])
        args = [mines[index] for index in range(first, first + count)]
        args.append((arrived, (tokens, rows), lambda i, blk: (0, jnp.maximum(i - count, 0))))
        if produced is not None:
            args.append((produced, None))

        def target(i, blk):
            return (0, blk[first + jnp.where(i < count, i, line + i - count)])

        return run_kernel(
            functools.partial(place_body, count=count),
            [((tokens, width), BF16, (tokens, rows), target)],
            args,
            grid=(2 * count,),
            scalars=(blocks,),
            aliases=None if produced is None else {len(args): 0},
        )[0]

    produced = place(1, line - 1, None)
    mines[0], theirs[0], up_grads[0] = close_block(
        0, (opened[0], after(more[0], up_ring[0], up_sums[1], produced))
    )
    produced = place(0, 1, produced)
    (down_own,) = run_kernel(
        functools.partial(ahead_body, scale=scale),
        [((rows, rank), F32)],
        [normed_ahead, act_ahead, after(down_grads[0][0], mines[3])],
    )
    up_sum = add(jnp.concatenate(up_ring, axis=0), up_grads[0])
    grads = jnp.concatenate([add(down_ring, down_own), up_sum], axis=1)
    return produced.reshape(1, micro, tok, width), grads[None]


def solution(mesh):
    def run(*args):
        rows = args[7].shape[1] // mesh.shape["rep"]
        split = mesh.shape["section"] == 4 and mesh.shape["rep"] == 8 and rows % 128 == 0
        body = per_device if split else plain_device
        return jax.shard_map(
            body,
            mesh=mesh,
            in_specs=(
                P("section", "rep", None, None),
                P("section", "rep", None, None),
                P("section", "rep", None),
                P("rep", None),
                P("rep", None, None),
                P("section", None),
                P("section", None),
                P("section", "rep", None),
                P("section", "rep", None),
            ),
            out_specs=(P("section", "rep", None, None), P("section", "rep", None)),
            check_vma=False,
        )(*args)

    return run
```

```python
import functools

import jax
import jax.numpy as jnp
from jax import lax
from jax.experimental import pallas as pl
from jax.experimental.pallas import tpu as pltpu
from jax.sharding import PartitionSpec as P

EPSILON = 1e-05
HALF_ROOT = 0.7071067811865476
DENSITY = 0.3989422804014327


def from_behind(value, axis, steps):
    count = lax.axis_size(axis)
    leading, last = (max(0, -steps), min(count, count - steps))
    return lax.ppermute(value, axis, [(source, source + steps) for source in range(leading, last)])


def unpack_codes(levels):
    return levels.astype(jnp.float32)


def gelu_pair(preact):
    normal_cdf = 0.5 * (1.0 + lax.erf(preact * HALF_ROOT))
    bump = DENSITY * jnp.exp(-0.5 * preact * preact)
    return (preact * normal_cdf, normal_cdf + preact * bump)


def section_inputs(stored, packed, scaling, picks):
    chosen = jnp.take(stored, picks, axis=0).astype(jnp.float32)
    rebuilt = chosen + scaling[..., None] * unpack_codes(packed)
    return rebuilt.astype(jnp.bfloat16).reshape(-1, stored.shape[-1])


def normalize(inputs, gain_row, bias_row):
    values = inputs.astype(jnp.float32)
    centred = values - jnp.mean(values, axis=-1, keepdims=True)
    inv_std = lax.rsqrt(jnp.mean(centred * centred, axis=-1, keepdims=True) + EPSILON)
    scaled = centred * inv_std
    normed = (scaled * gain_row + bias_row).astype(jnp.bfloat16)
    return (normed, scaled, inv_std)


def input_grad(out_grad, back, gain_row, scaled, inv_std):
    weighted = back * gain_row
    inner = (
        weighted
        - jnp.mean(weighted, axis=-1, keepdims=True)
        - scaled * jnp.mean(weighted * scaled, axis=-1, keepdims=True)
    )
    return (out_grad.astype(jnp.float32) + inv_std * inner).astype(jnp.bfloat16)


def contract_rows(left, right):
    return lax.dot_general(
        left, right, (((0,), (0,)), ((), ())), preferred_element_type=jnp.float32
    )


def contract_cols(left, right):
    return lax.dot_general(
        left, right, (((1,), (1,)), ((), ())), preferred_element_type=jnp.float32
    )


def take_rows(source, begin, count):
    return lax.dynamic_slice_in_dim(source, begin, count, 0)


def put_rows(target, active, values, begin):
    older = lax.dynamic_slice_in_dim(target, begin, values.shape[0], 0)
    return lax.dynamic_update_slice_in_dim(target, jnp.where(active, values, older), begin, 0)


def plain_device(
    history, codes, scales, sample_ids, cotangent, ln_gain, ln_bias, down_weight, up_weight
):
    sections = lax.axis_size("section")
    position = lax.axis_index("section")
    w_down, w_up = (
        lax.all_gather(down_weight[0], "rep", axis=0, tiled=True),
        lax.all_gather(up_weight[0], "rep", axis=0, tiled=True),
    )
    inputs = section_inputs(history[0], codes[0], scales[0], sample_ids[0])
    gain_row = ln_gain[0]
    bias_row = ln_bias[0]
    normed, scaled, inv_std = normalize(inputs, gain_row, bias_row)
    activated, slopes = gelu_pair(jnp.dot(normed, w_down, preferred_element_type=jnp.float32))
    hidden = activated.astype(jnp.bfloat16)
    tok_count = cotangent.shape[1]
    row_total = inputs.shape[0]
    model_width = inputs.shape[1]
    rank_pair = 2 * w_down.shape[1]
    seeded = cotangent.reshape(row_total, model_width)
    pieces = 1
    block_size = tok_count // pieces
    blocks = row_total // block_size
    tick_count = blocks + sections - 1

    def advance(tick, carry):
        incoming, produced, running, kept_grad, kept_top = carry
        offset = tick - (sections - 1 - position)
        active = jnp.logical_and(offset >= 0, offset < blocks)
        begin = jnp.clip(offset, 0, blocks - 1) * block_size
        top_grad = take_rows(seeded, begin, block_size)
        out_grad = jnp.where(position == sections - 1, top_grad, incoming)
        slope_rows = take_rows(slopes, begin, block_size)
        scaled_rows = take_rows(scaled, begin, block_size)
        inv_rows = take_rows(inv_std, begin, block_size)
        act_grad = (
            jnp.dot(out_grad, w_up, preferred_element_type=jnp.float32) * slope_rows
        ).astype(jnp.bfloat16)
        back = contract_cols(act_grad, w_down)
        result = input_grad(out_grad, back, gain_row, scaled_rows, inv_rows)
        produced = put_rows(produced, active, result, begin)
        normed_rows = take_rows(normed, begin, block_size)
        hidden_rows = take_rows(hidden, begin, block_size)
        terms = jnp.concatenate(
            [contract_rows(normed_rows, act_grad), contract_rows(out_grad, hidden_rows)], axis=1
        )
        running = running + jnp.where(active, terms, 0.0)
        incoming = from_behind(result, "section", -1)
        return (incoming, produced, running, kept_grad, kept_top)

    start_in = jnp.zeros((block_size, model_width), jnp.bfloat16)
    start_out = jnp.zeros((row_total, model_width), jnp.bfloat16)
    start_sum = jnp.zeros((model_width, rank_pair), jnp.float32)
    start_grad = jnp.zeros((1, 1), jnp.bfloat16)
    start_top = jnp.zeros((1, 1), jnp.bfloat16)
    carry = lax.fori_loop(
        0, tick_count, advance, (start_in, start_out, start_sum, start_grad, start_top)
    )
    produced = carry[1]
    summed = lax.psum_scatter(
        (carry[2] / float(tok_count)).astype(jnp.bfloat16), "rep", scatter_dimension=0, tiled=True
    ).astype(jnp.float32)
    return (produced.reshape(1, row_total // tok_count, tok_count, model_width), summed[None])


VMEM_LIMIT = 16 * 1024 * 1024
F32 = jnp.float32
BF16 = jnp.bfloat16


def run_kernel(body, outs, args, grid=(1,), scalars=(), scratch=(), aliases=None, limit=VMEM_LIMIT):
    def whole(shape):
        return pl.BlockSpec(shape, lambda *_: (0,) * len(shape))

    arrays, in_specs, out_specs, out_shapes = [], [], [], []
    for arg in args:
        if isinstance(arg, tuple) and arg[1] is None:
            arrays.append(arg[0])
            in_specs.append(pl.BlockSpec(memory_space=pltpu.HBM))
        elif isinstance(arg, tuple):
            arrays.append(arg[0])
            in_specs.append(pl.BlockSpec(arg[1], arg[2]))
        else:
            arrays.append(arg)
            in_specs.append(whole(arg.shape))
    for out in outs:
        out_shapes.append(jax.ShapeDtypeStruct(out[0], out[1]))
        out_specs.append(pl.BlockSpec(out[2], out[3]) if len(out) > 2 else whole(out[0]))
    return pl.pallas_call(
        body,
        out_shape=out_shapes,
        grid_spec=pltpu.PrefetchScalarGridSpec(
            num_scalar_prefetch=len(scalars),
            grid=grid,
            in_specs=in_specs,
            out_specs=out_specs,
            scratch_shapes=list(scratch),
        ),
        input_output_aliases=aliases or {},
        compiler_params=pltpu.CompilerParams(vmem_limit_bytes=limit),
        cost_estimate=pl.CostEstimate(flops=0, bytes_accessed=0, transcendentals=0),
    )(*scalars, *arrays)


def regroup_body(
    blocks, picks, hist0, hist1, code0, code1, cot0, cot1, step, own, sent, stats, kept, *, micro, tok
):
    place = pl.program_id(0)
    last = pl.num_programs(0) - 1

    @pl.when(place < last)
    def _():
        for which, (hist, code, cot, out) in enumerate(
            ((hist0, code0, cot0, own), (hist1, code1, cot1, sent))
        ):
            for m in range(micro):
                rows = pl.ds(m * tok, tok)
                rebuilt = hist[picks[m]].astype(F32) + step[m] * code[m].astype(F32)
                rebuilt = rebuilt.astype(BF16)
                out[0, rows, :] = rebuilt
                out[1, rows, :] = cot[m]
                kept[2 * place + which, rows, :] = rebuilt

    @pl.when(place == last)
    def _():
        total, rows, lanes = kept.shape
        width = total * lanes

        def add(index, acc):
            return acc + jnp.sum(kept[index].astype(F32), axis=-1, keepdims=True)

        mean = lax.fori_loop(0, total, add, jnp.zeros((rows, 1), F32)) / width

        def add_square(index, acc):
            centred = kept[index].astype(F32) - mean
            return acc + jnp.sum(centred * centred, axis=-1, keepdims=True)

        var = lax.fori_loop(0, total, add_square, jnp.zeros((rows, 1), F32)) / width
        inv_std = lax.rsqrt(var + EPSILON)
        half = stats.shape[1] // 2
        stats[:, :half] = jnp.broadcast_to(mean, (rows, half))
        stats[:, half:] = jnp.broadcast_to(inv_std, (rows, half))
        lane = lax.broadcasted_iota(jnp.int32, (rows, 128), 1)
        packed = jnp.zeros((rows, 128), F32)
        for index, value in enumerate(bf16_parts(mean) + bf16_parts(inv_std)):
            packed = jnp.where(lane == index, value, packed)
        sent[0, :, :128] = packed.astype(BF16)


def bf16_parts(value):
    parts = []
    for _ in range(3):
        parts.append(value.astype(BF16).astype(F32))
        value = value - parts[-1]
    return parts


def split_stats(stats):
    if len(stats.shape) == 3:
        parts = stats[0].astype(F32)
        return [sum(parts[:, i : i + 1] for i in range(k, k + 3)) for k in (0, 3)]
    half = stats.shape[1] // 2
    return stats[:, 0:1], stats[:, half : half + 1]


def norm_body(blocks, own, sib, stats_own, stats_sib, gain, bias, out):
    tokens = own.shape[1]
    for slot, (values, stats) in enumerate(((own, stats_own), (sib, stats_sib))):
        mean, inv_std = split_stats(stats)
        scaled = (values[0].astype(F32) - mean) * inv_std
        out[slot * tokens : (slot + 1) * tokens, :] = (scaled * gain[...] + bias[...]).astype(BF16)


def as_column(row, lanes):
    turned = jnp.transpose(jnp.broadcast_to(row, (128, row.shape[1])))
    return jnp.concatenate([turned] * (lanes // 128), axis=1)


def step_body(*refs, first, sections):
    refs = refs[1:]
    own, sib, stats_own, stats_sib, gain, bias, down, up, near, far, diag_a, diag_b = refs[:12]
    refs = refs[12:]
    if first:
        old = None
        outs = refs
    else:
        old, outs = refs[:3], refs[3:]
    rank = down.shape[1]
    tokens = own.shape[1]
    weights = down[...]
    gain_row, bias_row = gain[...], bias[...]
    others = [near[...], far[...], jnp.concatenate([diag_a[...], diag_b[...]], axis=0)]
    for slot, (values, stats) in enumerate(((own, stats_own), (sib, stats_sib))):
        mean, inv_std = split_stats(stats)
        inputs = values[0]
        scaled = (inputs.astype(F32) - mean) * inv_std
        normed = (scaled * gain_row + bias_row).astype(BF16)
        pieces = [
            jnp.dot(values[1], up[...], preferred_element_type=F32),
            jnp.dot(normed, weights, preferred_element_type=F32),
        ] + [jnp.dot(inputs, other, preferred_element_type=F32) for other in others]
        for index, piece in enumerate(pieces):
            columns = slice(index * rank, (index + 1) * rank)
            if old is not None:
                piece = piece + old[slot][:, columns]
            outs[slot][:, columns] = piece
    wide = weights.astype(F32)
    gained = wide * as_column(gain_row, rank)
    biased = wide * as_column(bias_row, rank)
    gained_low = gained.astype(BF16)
    cross = outs[2]

    def put(rows, columns, value):
        if old is not None:
            value = value + old[2][rows, columns]
        cross[rows, columns] = value

    for index, other in enumerate(others):
        columns = slice(index * rank, (index + 1) * rank)
        put(slice(0, rank), columns, contract_rows(gained_low, other))
        put(
            slice(rank, rank + 1),
            columns,
            jnp.sum(other.astype(F32), axis=0, keepdims=True),
        )
    put(slice(rank + 1, rank + 2), slice(0, rank), jnp.sum(gained, axis=0, keepdims=True))
    put(slice(rank + 1, rank + 2), slice(rank, 2 * rank), jnp.sum(biased, axis=0, keepdims=True))


def chain_values(pre, slopes, centred, spread, cross, kappa, inv_std, width):
    act_grad = (pre * slopes).astype(BF16)
    wide = act_grad.astype(F32)
    second = jnp.sum(wide * centred, axis=-1, keepdims=True) / width
    return inv_std * (jnp.dot(act_grad, cross, preferred_element_type=F32) - second * spread)


def open_body(
    mine, got, cross, cross_got, stats, small, shared, spread_out, cross_out, kappa_out, near, rest, *, width
):
    rank = near.shape[1]
    total = mine[...] + got[...]
    both = cross[...] + cross_got[...]
    mean, inv_std = split_stats(stats)
    base = total[:, :rank]
    preact = total[:, rank : 2 * rank]
    sums = both[rank : rank + 1, :]
    kappa = both[rank + 1 : rank + 2, :rank]
    beta = both[rank + 1 : rank + 2, rank : 2 * rank]
    activated, slopes = gelu_pair(preact)
    centred = preact - beta
    spread = inv_std * (total[:, 2 * rank :] - mean * sums)
    kappa_column = as_column(kappa, rank)[:, 0:1]
    projected = (both[:rank, :] - kappa_column * (sums / width)).astype(BF16)
    small[:, :rank] = base
    small[:, rank:] = slopes
    shared[:, :rank] = activated
    shared[:, rank:] = centred
    spread_out[...] = spread
    cross_out[...] = projected
    kappa_out[...] = jnp.broadcast_to(kappa, kappa_out.shape)
    values = chain_values(base, slopes, centred, spread, projected, kappa, inv_std, width)
    near[...] = values[:, :rank].astype(BF16)
    rest[...] = values[:, rank:].astype(BF16)


def chain_body(*refs, width, turn):
    small, shared, spread, cross, kappa, stats = refs[:6]
    arrivals, out = refs[6:-1], refs[-1]
    rank = cross.shape[0]
    _, inv_std = split_stats(stats)
    pre = small[:, :rank]
    for arrival in arrivals:
        pre = pre + arrival[:, :rank].astype(F32)
    slopes = small[:, rank:]
    if turn == 3:
        out[...] = (pre * slopes).astype(BF16)
        return
    values = chain_values(
        pre, slopes, shared[:, rank:], spread[...], cross[...], kappa[0:1, :], inv_std, width
    )
    if turn == 1:
        out[:, :rank] = values[:, 2 * rank :].astype(BF16)
        out[:, rank:] = values[:, rank : 2 * rank].astype(BF16)
        return
    passed = arrivals[1][:, rank:].astype(F32) + arrivals[2][:, rank:].astype(F32)
    out[...] = (values[:, :rank] + passed).astype(BF16)


def grad_body(*refs, scale, width, index):
    *refs, held, sems = refs
    columns = pl.ds(index * held.shape[2], held.shape[2])
    copies = [
        pltpu.make_async_copy(source.at[0, :, columns], held.at[slot], sems.at[slot])
        for slot, source in enumerate(refs[1:3])
    ]
    for copy in copies:
        copy.start()
    stats_own, stats_sib, act_own, act_sib, shared_own, shared_sib, kappa = refs[3:10]
    gain, bias, down, term, *grads = refs[10:]
    gain_row, bias_row = gain[...], bias[...]
    weights = down[...]
    rank = weights.shape[1]
    total = None
    for slot, (stats, act, shared) in enumerate(
        ((stats_own, act_own, shared_own), (stats_sib, act_sib, shared_sib))
    ):
        mean, inv_std = split_stats(stats)
        act_grad = act[...]
        wide = act_grad.astype(F32)
        first = jnp.sum(wide * kappa[0:1, :], axis=-1, keepdims=True) / width
        second = jnp.sum(wide * shared[:, rank:], axis=-1, keepdims=True) / width
        copies[slot].wait()
        scaled = (held[slot].astype(F32) - mean) * inv_std
        normed = (scaled * gain_row + bias_row).astype(BF16)
        weighted = contract_cols(act_grad, weights) * gain_row
        tokens = act_grad.shape[0]
        term[slot * tokens : (slot + 1) * tokens, :] = (
            inv_std * (weighted - first - scaled * second)
        ).astype(BF16)
        piece = contract_rows(normed, act_grad)
        total = piece if total is None else total + piece
    for grad in grads:
        grad[...] = (total * scale).astype(BF16)


def ahead_body(normed, act, own, out, *, scale):
    out[...] = own[...].astype(F32) + contract_rows(normed[...], act[...]) * scale


def close_body(*refs, scale, count, index):
    *refs, held, sems = refs
    columns = pl.ds(index * held.shape[2], held.shape[2])
    copies = [
        pltpu.make_async_copy(source.at[1, :, columns], held.at[slot], sems.at[slot])
        for slot, source in enumerate(refs[1:3])
    ]
    for copy in copies:
        copy.start()
    level, _, _, shared_own, shared_sib, term = refs[0:6]
    arrivals = refs[6 : 6 + count]
    mine, theirs, grad = refs[6 + count :]
    rank = grad.shape[1]
    total = None
    for slot, (shared, out) in enumerate(((shared_own, mine), (shared_sib, theirs))):
        tokens = shared.shape[0]
        rows = slice(slot * tokens, (slot + 1) * tokens)
        copies[slot].wait()
        arrived = held[slot].astype(F32)
        for place, arrival in enumerate(arrivals):
            values = arrival[rows, :].astype(F32)
            if place == 0:
                values = jnp.where(level[0] % 2 == 0, values, 0.0)
            arrived = arrived + values
        out_grad = arrived.astype(BF16)
        out[...] = (out_grad.astype(F32) + term[rows, :].astype(F32)).astype(BF16)
        piece = contract_rows(out_grad, shared[:, :rank].astype(BF16))
        total = piece if total is None else total + piece
    grad[...] = (total * scale).astype(BF16)


def place_body(blocks, *refs, count):
    mines, arrived, out = refs[:count], refs[count], refs[-1]
    place = pl.program_id(0)
    for index, source in enumerate(mines):

        @pl.when(place == index)
        def _():
            out[...] = source[...]

    @pl.when(place >= count)
    def _():
        out[...] = arrived[...]


def per_device(
    history, codes, scales, sample_ids, cotangent, ln_gain, ln_bias, down_weight, up_weight
):
    sections = lax.axis_size("section")
    reps = lax.axis_size("rep")
    line = reps // 2
    section = lax.axis_index("section")
    rep = lax.axis_index("rep")
    chip, core = rep // 2, rep % 2
    _, micro, tok, width = history.shape
    tokens = micro * tok
    rows, rank = down_weight.shape[1:]

    def sibling(value):
        return lax.ppermute(value, "rep", [(r, r ^ 1) for r in range(reps)])

    def along(value, steps=1):
        return lax.ppermute(value, "rep", [(r, (r + 2 * steps) % reps) for r in range(reps)])

    def flip(value, mask):
        return lax.ppermute(value, "section", [(s, s ^ mask) for s in range(sections)])

    def after(value, *first):
        return lax.optimization_barrier((value, first))[0]

    chips = (chip - jnp.arange(line, dtype=jnp.int32)) % line
    blocks = jnp.concatenate([2 * chips + core, 2 * chips + 1 - core]).astype(jnp.int32)
    gain, bias = ln_gain, ln_bias

    ups, downs = [up_weight[0]], [down_weight[0]]
    cut = rows // 2

    def both(value):
        return flip(value, 1), flip(value, 2)

    def first_half(near, *first):
        return flip(after(near, *first)[:cut], 2)

    def second_half(far, *first):
        return flip(after(far, *first)[cut:], 1)

    nears = [both(ups[0])]
    ups.append(along(ups[0]))

    def columns(kind):
        return lambda i, blk, ids: (0, 0, blk[kind * line + jnp.minimum(i, line - 1)])

    own, sent, stats = run_kernel(
        functools.partial(regroup_body, micro=micro, tok=tok),
        [
            (
                (2, tokens, line * rows),
                BF16,
                (2, tokens, rows),
                lambda i, *_: (0, 0, jnp.minimum(i, line - 1)),
            ),
            ((2, tokens, (line + 1) * rows), BF16, (2, tokens, rows), lambda i, *_: (0, 0, i)),
            ((tokens, 256), F32),
        ],
        [
            (value, (micro, tok, rows), columns(kind))
            for value in (history[0], codes[0], cotangent)
            for kind in (0, 1)
        ]
        + [scales[0][..., None]],
        grid=(line + 1,),
        scalars=(blocks, sample_ids[0]),
        scratch=[pltpu.VMEM((2 * line, tokens, rows), BF16)],
    )
    sib = sibling(after(sent, *nears[0], ups[1]))
    stats_sib = (sib, (1, tokens, 128), lambda i, *_: (0, 0, line * rows // 128))

    ups.append(along(ups[1]))
    downs.append(along(after(downs[0], ups[1])))
    nears.append(both(ups[1]))
    def part(value, index):
        return (value, (2, tokens, rows), lambda i, *_: (0, 0, index))

    def one(value, kind, index):
        return (value, (1, tokens, rows), lambda i, *_: (kind, 0, index))

    def feature(value, index):
        return (value, (1, rows), lambda i, blk: (0, blk[index]))

    def add_step(sums, index, gathered):
        first = index == 0
        args = [
            part(own, index),
            part(sib, index),
            stats,
            stats_sib,
            feature(gain, index),
            feature(bias, index),
            downs[index],
            ups[index],
            *gathered,
        ]
        shapes = [
            ((tokens, (1 + sections) * rank), F32),
            ((tokens, (1 + sections) * rank), F32),
            ((rank + 8, (sections - 1) * rank), F32),
        ]
        return run_kernel(
            functools.partial(step_body, first=first, sections=sections),
            shapes,
            args + list(sums),
            scalars=(blocks,),
            aliases=None if first else {13 + i: i for i in range(3)},
            limit=28 * 1024 * 1024,
        )

    firsts = [first_half(nears[0][0], *nears[1])]
    ups.append(along(ups[2]))
    downs.append(along(downs[1]))
    nears.append(both(after(ups[2], *nears[1], sib)))
    seconds = [second_half(nears[0][1], *nears[2])]
    firsts.append(first_half(nears[1][0], *nears[2]))
    seconds.append(second_half(nears[1][1], *nears[2]))
    sums = add_step((), 0, nears[0] + (firsts[0], seconds[0]))
    nears.append(both(after(ups[3], *nears[2], *firsts, *seconds, *sums)))
    for index in range(2, line):
        firsts.append(first_half(nears[index][0]))
        seconds.append(second_half(nears[index][1]))
    (normed,) = run_kernel(
        norm_body,
        [((2 * tokens, rows), BF16)],
        [
            one(own, 0, 1),
            one(sib, 0, 1),
            stats,
            stats_sib,
            feature(gain, 1),
            feature(bias, 1),
        ],
        scalars=(blocks,),
    )
    downs.append(along(downs[2]))
    for index in range(1, line):
        sums = add_step(after(sums, normed), index, nears[index] + (firsts[index], seconds[index]))
    mine, other, cross = sums
    normed_ahead = along(after(normed, mine), -1)

    got, cross_got = sibling(other), sibling(cross)

    apart = sections - 1
    small, shared, spread, projected, kappa, to_next, to_rest = run_kernel(
        functools.partial(open_body, width=width),
        [
            ((tokens, 2 * rank), F32),
            ((tokens, 2 * rank), F32),
            ((tokens, apart * rank), F32),
            ((rank, apart * rank), BF16),
            ((8, rank), F32),
            ((tokens, rank), BF16),
            ((tokens, 2 * rank), BF16),
        ],
        [mine, got, cross, cross_got, stats],
    )
    arrivals = [lax.ppermute(to_next, "section", [(3, 2)])]
    late = lax.ppermute(to_rest, "section", [(3, 1)])
    state = [small, shared, spread, projected, kappa, stats]
    for turn in (1, 2, 3):
        (passed,) = run_kernel(
            functools.partial(chain_body, width=width, turn=turn),
            [((tokens, 2 * rank if turn == 1 else rank), BF16)],
            state + arrivals,
        )
        if turn == 1:
            arrivals += [late, lax.ppermute(passed, "section", [(2, 1)])]
        elif turn == 2:
            arrivals += [lax.ppermute(passed, "section", [(1, 0)])]
    act = passed
    act_sib, shared_sib = sibling(act), sibling(shared)

    scale = 1.0 / tok
    level = section.astype(jnp.int32).reshape(1)

    def grad_block(index, act):
        outs = [((2 * tokens, rows), BF16)]
        if index != 1:
            outs.append(((rows, rank), BF16))
        return run_kernel(
            functools.partial(grad_body, scale=scale, width=width, index=index),
            outs,
            [
                (own, None),
                (sib, None),
                stats,
                stats_sib,
                act,
                act_sib,
                shared,
                shared_sib,
                kappa,
                feature(gain, index),
                feature(bias, index),
                downs[index],
            ],
            scalars=(blocks,),
            scratch=[pltpu.VMEM((2, tokens, rows), BF16), pltpu.SemaphoreType.DMA((2,))],
        )

    def close_block(index, arrived):
        return run_kernel(
            functools.partial(close_body, scale=scale, count=len(arrived), index=index),
            [((tokens, rows), BF16), ((tokens, rows), BF16), ((rows, rank), BF16)],
            [(own, None), (sib, None), shared, shared_sib, terms[index], *arrived],
            scalars=(level,),
            scratch=[pltpu.VMEM((2, tokens, rows), BF16), pltpu.SemaphoreType.DMA((2,))],
        )

    terms, down_grads, up_grads, mines, theirs = {}, {}, {}, {}, {}
    act_sib = after(act_sib, normed_ahead)
    (terms[1],) = grad_block(1, act)
    act = after(act, terms[1])
    terms[2], *down_grads[2] = grad_block(2, act)
    terms[3], *down_grads[3] = grad_block(3, act)

    def add(*values):
        return sum(value.astype(F32) for value in values)

    def pass_on(running, part):
        return along(add(running, part).astype(BF16))

    def scan_open(index):
        return lax.ppermute(terms[index], "section", [(3, 2), (1, 0), (2, 3)])

    def scan_pairs(*pairs):
        return lax.ppermute(terms[1], "section", pairs)

    def scan_sum(index, arrived):
        return add(terms[index], arrived).astype(BF16)

    def scan_more(value):
        return lax.ppermute(value, "section", [(3, 1), (2, 0)])

    opened = {1: scan_pairs((3, 2), (2, 3))}
    beside = scan_pairs((1, 0))
    opened.update({index: scan_open(index) for index in (2, 3)})
    down_ring = along(down_grads[2][0])
    sums = {1: scan_sum(1, after(opened[1], terms[2], terms[3]))}
    more = {1: scan_more(sums[1])}
    down_sum = add(after(down_ring, beside), down_grads[3][0]).astype(BF16)
    down_ring = along(down_sum)
    sums[2] = scan_sum(2, after(opened[2], more[1]))
    more[2] = scan_more(sums[2])
    mines[1], theirs[1], up_grads[1] = close_block(
        1, (opened[1], after(more[1], down_sum, sums[2]), beside)
    )
    up_ring = along(up_grads[1])
    terms[0], *down_grads[0] = grad_block(0, after(act, up_grads[1]))
    opened[0] = scan_open(0)
    sums[3] = scan_sum(3, after(opened[3], sums[2], up_grads[1]))
    more[3] = scan_more(sums[3])
    mines[2], theirs[2], up_grads[2] = close_block(
        2, (opened[2], after(more[2], sums[3], down_ring))
    )
    more[0] = scan_more(scan_sum(0, after(opened[0], sums[3], up_grads[2])))
    halves = [slice(0, rows // 2), slice(rows // 2, rows)]
    up_sums = [add(up_ring[half], up_grads[2][half]).astype(BF16) for half in halves]
    up_ring = [along(value) for value in up_sums]
    mines[3], theirs[3], up_grads[3] = close_block(3, (opened[3], after(more[3], *up_sums)))
    up_sums = [add(up_ring[0], up_grads[3][halves[0]]).astype(BF16)]
    act_ahead = along(jnp.concatenate(after([act, act_sib], up_sums[0]), axis=0), -1)
    second = after(up_ring[1], up_sums[0])
    up_sums.append(add(second, up_grads[3][halves[1]]).astype(BF16))
    up_ring = [along(value) for value in up_sums]

    def place(first, count, produced):
        sent = [theirs[index] for index in range(first, first + count)]
        arrived = sibling(jnp.concatenate(sent, axis=1) if count > 1 else sent[0])
        args = [mines[index] for index in range(first, first + count)]
        args.append((arrived, (tokens, rows), lambda i, blk: (0, jnp.maximum(i - count, 0))))
        if produced is not None:
            args.append((produced, None))

        def target(i, blk):
            return (0, blk[first + jnp.where(i < count, i, line + i - count)])

        return run_kernel(
            functools.partial(place_body, count=count),
            [((tokens, width), BF16, (tokens, rows), target)],
            args,
            grid=(2 * count,),
            scalars=(blocks,),
            aliases=None if produced is None else {len(args): 0},
        )[0]

    produced = place(1, line - 1, None)
    mines[0], theirs[0], up_grads[0] = close_block(
        0, (opened[0], after(more[0], up_ring[0], up_sums[1], produced))
    )
    produced = place(0, 1, produced)
    (down_own,) = run_kernel(
        functools.partial(ahead_body, scale=scale),
        [((rows, rank), F32)],
        [normed_ahead, act_ahead, after(down_grads[0][0], mines[3])],
    )
    up_sum = add(jnp.concatenate(up_ring, axis=0), up_grads[0])
    grads = jnp.concatenate([add(down_ring, down_own), up_sum], axis=1)
    return produced.reshape(1, micro, tok, width), grads[None]


def solution(mesh):
    def run(*args):
        rows = args[7].shape[1] // mesh.shape["rep"]
        split = mesh.shape["section"] == 4 and mesh.shape["rep"] == 8 and rows % 128 == 0
        body = per_device if split else plain_device
        return jax.shard_map(
            body,
            mesh=mesh,
            in_specs=(
                P("section", "rep", None, None),
                P("section", "rep", None, None),
                P("section", "rep", None),
                P("rep", None),
                P("rep", None, None),
                P("section", None),
                P("section", None),
                P("section", "rep", None),
                P("section", "rep", None),
            ),
            out_specs=(P("section", "rep", None, None), P("section", "rep", None)),
            check_vma=False,
        )(*args)

    return run
```
